512 devices in a mesh: depth: 16 (over y, core), tile: 32 (over z, x).
Axes of the slice: x: 4, y: 8, z: 8, core: 2. Of those that a mesh axis runs over, the one named last changes fastest.
Arguments:
- colour: bfloat16 [16, 3, 4096, 4096], P('depth', None, 'tile'), may hold values from -6 to 6
- alpha: bfloat16 [16, 4096, 4096], P('depth', 'tile'), may hold values from 0.049804688 to 0.5
- depth_order: int32 [16], replicated, may hold values from 0 to 15, as said below
- row_taps: int32 [4, 4096], P(None, 'tile'), may hold values from 0 to 383, as said below
- row_weights: bfloat16 [4, 4096], P(None, 'tile'), may hold values from -0.25 to 0.75
- col_taps: int32 [4, 4, 4096], P(None, None, 'depth'), may hold values from 0 to 4095, as said below
- col_weights: bfloat16 [4, 4, 4096], P(None, None, 'depth'), may hold values from -0.25 to 0.75
- colour_matrix: float32 [4, 3, 3], replicated
- offsets: float32 [4, 3], replicated, may hold values from -0.5 to 0.5
Outputs:
- projected: float32 [3, 4096, 4096], P(None, 'tile', 'depth')
The draws below stay inside these ranges and needn't reach their ends.
Inputs may be any that keep to these rules, and one draw needn't show every extreme that they name: depth_order[k] = f XOR b(k), where b(k) reverses the order of the bits of k over the 16 values and f is one number of 0 to 15: the groups are the leaves of a binary space partition, visited front to back. `row_taps`: the four taps of an output row are consecutive rows, rising by one; within a band the first tap minus the output row's place in its band is the same for all rows. `col_taps`: the four taps of an output column x are consecutive columns, rising by one, all within 128 columns of x.
All inputs are finite; a program needn't handle non-finite values.
Results may differ from the reference program's by a relative error of at most 0.0038.
Values may be sent and summed in bfloat16 or wider, within the bound.
A program may use at most 64 MiB of HBM per device.

```python
import jax
import jax.numpy as jnp
from jax import lax

ROWS = 128
COLS = 4096
HC = 128
BANDS = 8
BLEND = 64
GROUPS = 16
H = 4096
PROJ = 4


def draw_depth_order(key, part):
    levels = GROUPS.bit_length() - 1
    flip_bits = jax.random.randint(jax.random.fold_in(key, 5), (), 0, GROUPS)
    positions = jnp.arange(GROUPS)
    reversed_bits = jnp.zeros((GROUPS,), jnp.int32)
    for level in range(levels):
        reversed_bits = reversed_bits + ((positions >> level & 1) << levels - 1 - level)
    return (reversed_bits ^ flip_bits).astype(jnp.int32)


def draw_row_taps(key, part):
    key_a = jax.random.fold_in(key, 11)
    bands_total = H // ROWS
    band_ids = jnp.arange(bands_total)
    offset_rows = jax.random.randint(key_a, (bands_total,), -1, 1)
    offset_rows = jnp.where(band_ids == 0, -(ROWS - 1), offset_rows)
    offset_rows = jnp.where(band_ids == bands_total - 1, ROWS - 2, offset_rows)
    position = ROWS + jnp.arange(ROWS)[None, :] + offset_rows[:, None]
    tap_rows = position[None, :, :] + jnp.arange(-1, 3)[:, None, None]
    return tap_rows.reshape(4, H).astype(jnp.int32)


def draw_col_taps(key, part):
    key_a, key_b, key_c = jax.random.split(jax.random.fold_in(key, 23), 3)
    proj_ids = jnp.arange(PROJ)
    limit = HC // 2 - 4
    chosen = jax.random.randint(key_c, (), 0, PROJ)
    offset_x = jax.random.randint(key_a, (PROJ,), -limit, limit + 1)
    offset_x = jnp.where(proj_ids == chosen, 0, offset_x)
    slope_x = jax.random.randint(key_b, (PROJ,), -limit, limit + 1)
    slope_x = jnp.where(proj_ids == chosen, 0, slope_x)
    column = jnp.arange(COLS)[None, :]
    position = jnp.clip(column + offset_x[:, None] + column * slope_x[:, None] // COLS, 1, COLS - 3)
    tap_cols = position[:, None, :] + jnp.arange(-1, 3)[None, :, None]
    return tap_cols.astype(jnp.int32)


def draw_colour_matrix(key, part):
    key_a = jax.random.fold_in(key, 37)
    spread = jnp.clip(0.15 * jax.random.normal(key_a, (PROJ, 3, 3), jnp.float32), -0.35, 0.35)
    return (jnp.eye(3, dtype=jnp.float32)[None] + spread).astype(jnp.float32)


def steps_of(stream_key, shape, cuts, least, largest):
    def one(dim, shards_of):
        steps = jax.random.uniform(jax.random.fold_in(jax.random.fold_in(stream_key, 6), dim), (shards_of,), jnp.float32, least / len(cuts), largest / len(cuts))
        return jnp.repeat(jnp.exp(steps), shape[dim] // shards_of).reshape((-1,) + (1,) * (len(shape) - dim - 1))

    gain = one(*cuts[0])
    for cut in cuts[1:]:
        gain = gain * one(*cut)
    return gain


def bell_draw(key, extent, deviation, most, shards=(), kind=jnp.bfloat16):
    gain = steps_of(key, extent, shards, -0.22, 0.18) if shards else 1.0
    entries = jax.random.normal(key, extent, jnp.float32) * deviation * gain
    return jnp.minimum(jnp.maximum(entries, -most), most).astype(kind)


def setup_inputs(seed: int = 0) -> dict:
    keys = jax.random.split(jax.random.key(seed), 10)
    colour = bell_draw(keys[0], (GROUPS, 3, H, COLS), 1.0, 6.0, ((0, 16), (2, 32)))
    alpha = jnp.clip(0.049804688 + 0.4501953 * jax.random.uniform(keys[1], (GROUPS, H, COLS), jnp.float32) ** steps_of(keys[1], (GROUPS, H, COLS), ((0, 16), (1, 32)), -0.2, 0.2), 0.049804688, 0.5).astype(jnp.bfloat16)
    depth_order = draw_depth_order(jax.random.fold_in(keys[9], 71), 0)
    row_taps = draw_row_taps(jax.random.fold_in(keys[9], 71), 0)
    row_weights = jnp.clip(-0.25 + 1.0 * jax.random.uniform(keys[4], (4, H), jnp.float32) ** steps_of(keys[4], (4, H), ((1, 32),), -0.2, 0.2), -0.25, 0.75).astype(jnp.bfloat16)
    col_taps = draw_col_taps(jax.random.fold_in(keys[9], 71), 0)
    col_weights = jnp.clip(-0.25 + 1.0 * jax.random.uniform(keys[6], (PROJ, 4, COLS), jnp.float32) ** steps_of(keys[6], (PROJ, 4, COLS), ((2, 16),), -0.2, 0.2), -0.25, 0.75).astype(jnp.bfloat16)
    colour_matrix = draw_colour_matrix(jax.random.fold_in(keys[9], 71), 0)
    offsets = jnp.clip(jax.random.uniform(keys[8], (PROJ, 3), jnp.float32, -0.5, 0.5), -0.5, 0.5)
    return {"colour": colour, "alpha": alpha, "depth_order": depth_order, "row_taps": row_taps, "row_weights": row_weights, "col_taps": col_taps, "col_weights": col_weights, "colour_matrix": colour_matrix, "offsets": offsets}


def reference(colour, alpha, depth_order, row_taps, row_weights, col_taps, col_weights, colour_matrix, offsets):
    accumulated = jnp.zeros((3, H, COLS), jnp.float32)
    remaining = jnp.ones((H, COLS), jnp.float32)
    for position in range(GROUPS):
        group_id = depth_order[position]
        layer_colour = lax.dynamic_index_in_dim(colour, group_id, 0, keepdims=False).astype(jnp.float32)
        layer_alpha = lax.dynamic_index_in_dim(alpha, group_id, 0, keepdims=False).astype(jnp.float32)
        accumulated = accumulated + remaining[None] * layer_colour
        remaining = remaining * (1.0 - layer_alpha)
    composite = accumulated.astype(jnp.bfloat16)
    padded = jnp.pad(composite, ((0, 0), (ROWS, ROWS), (0, 0)))
    bands_total = H // ROWS
    tap_rows_all = jnp.transpose(row_taps.reshape(4, bands_total, ROWS), (1, 0, 2))
    weight_rows_all = jnp.transpose(row_weights.reshape(4, bands_total, ROWS), (1, 0, 2))
    row_index = jnp.arange(ROWS).astype(jnp.float32)
    proj_height = BANDS * ROWS

    def band_work(band_items):
        band_index, tap_rows, weight_rows = band_items
        proj_index = band_index // BANDS
        tap_cols = lax.dynamic_index_in_dim(col_taps, proj_index, 0, keepdims=False)
        weight_cols = lax.dynamic_index_in_dim(col_weights, proj_index, 0, keepdims=False)
        colour_mix = lax.dynamic_index_in_dim(colour_matrix, proj_index, 0, keepdims=False)
        colour_shift = lax.dynamic_index_in_dim(offsets, proj_index, 0, keepdims=False)
        window = lax.dynamic_slice_in_dim(padded, (band_index * ROWS).astype(jnp.int32), 3 * ROWS, 1)
        vertical = jnp.zeros((3, ROWS, COLS), jnp.float32)
        for tap_index in range(4):
            vertical = vertical + weight_rows[tap_index].astype(jnp.float32)[None, :, None] * window[:, tap_rows[tap_index], :].astype(jnp.float32)
        vertical = vertical.astype(jnp.bfloat16)
        warped = jnp.zeros((3, ROWS, COLS), jnp.float32)
        for tap_index in range(4):
            warped = warped + weight_cols[tap_index].astype(jnp.float32)[None, None, :] * vertical[:, :, tap_cols[tap_index]].astype(jnp.float32)
        within = ((band_index % BANDS) * ROWS).astype(jnp.float32) + row_index
        blend_ramp = jnp.minimum(1.0, jnp.minimum((within + 0.5) / BLEND, (proj_height - within - 0.5) / BLEND))
        blended = warped * blend_ramp[None, :, None]
        outputs = []
        for channel in range(3):
            mixed_sum = colour_mix[channel, 0] * blended[0] + colour_mix[channel, 1] * blended[1] + colour_mix[channel, 2] * blended[2]
            outputs.append(mixed_sum + colour_shift[channel])
        return jnp.stack(outputs)

    stacked = lax.map(band_work, (jnp.arange(bands_total).astype(jnp.int32), tap_rows_all, weight_rows_all))
    return jnp.transpose(stacked, (1, 0, 2, 3)).reshape(3, H, COLS)
```

```python
import functools

import jax
import jax.numpy as jnp
from jax import lax
from jax.experimental import pallas as pl
from jax.experimental.pallas import tpu as pltpu
from jax.sharding import PartitionSpec as P

HC = 128
BLEND = 64
GROUPS = 16
CHIPS = 8
CHUNKS = 4
TILE_ROWS = 16
LANES = 128
STEPS = (4, 5, 3, 6, 2, 7, 1)
MESH = pl.DeviceIdType.MESH
F32 = jnp.float32
BF16 = jnp.bfloat16


def square(x):
    return (x * jnp.abs(x)).astype(BF16)


def root(v):
    v = v.astype(F32)
    return v * lax.rsqrt(jnp.maximum(jnp.abs(v), 1e-37))


def kernel(
    bands_per_projector,
    tiles,
    colour, alpha, order, row_taps, row_weights, col_taps, col_weights, matrix, offsets,
    out,
    opac, cols, remain_out, remain_in, part_out, part_in, window, low, vert,
    a_send, a_recv, a_own, c_own, c_send, c_recv, r_send, r_recv, p_send, p_recv,
    h_send, h_recv, v_send, v_recv,
):
    height, slab = out.shape[1], out.shape[2]
    chunk = height // CHUNKS
    blocks = (chunk // TILE_ROWS) * (slab // LANES)
    d = lax.axis_index("depth")
    t = lax.axis_index("tile")
    y, c = d // 2, d % 2
    sigma = 1 - 2 * c
    sibling = 2 * y + 1 - c
    below, above = (t + 1) % tiles, (t + tiles - 1) % tiles

    def chip(offset):
        return (y + offset + 2 * CHIPS) % CHIPS

    def columns(device):
        return pl.ds(pl.multiple_of(device * slab, slab), slab)

    def rows_of(k):
        return pl.ds(pl.multiple_of(k * chunk, chunk), chunk)

    barrier = pltpu.get_barrier_semaphore()

    def greet(i, _):
        pl.semaphore_signal(barrier, 1, device_id=((d + i) % GROUPS, t), device_id_type=MESH)
        return 0

    lax.fori_loop(1, GROUPS, greet, 0)
    pl.semaphore_signal(barrier, 1, device_id=(d, below), device_id_type=MESH)
    pl.semaphore_signal(barrier, 1, device_id=(d, above), device_id_type=MESH)

    def own_alpha(k):
        return pltpu.make_async_copy(
            alpha.at[0, rows_of(k), columns(d)], opac.at[k, d], a_own.at[k]
        )

    def own_colour(s):
        return pltpu.make_async_copy(
            colour.at[0, :, :, columns(2 * s + c)], cols.at[c, s], c_own.at[s]
        )

    def loop(n, body):
        def step(i, _):
            body(i)
            return 0

        lax.fori_loop(0, n, step, 0)

    loop(CHUNKS, lambda k: own_alpha(k).start())
    loop(CHIPS, lambda s: own_colour(s).start())
    pl.semaphore_wait(barrier, GROUPS + 1)

    def send_alpha(k, i):
        to = (d + i) % GROUPS
        return pltpu.make_async_remote_copy(
            src_ref=alpha.at[0, rows_of(k), columns(to)],
            dst_ref=opac.at[k, d],
            send_sem=a_send.at[k, i],
            recv_sem=a_recv.at[k, i],
            device_id=(to, t),
            device_id_type=MESH,
        )

    def recv_alpha(k, i):
        source = (d + GROUPS - i) % GROUPS
        return pltpu.make_async_remote_copy(
            src_ref=alpha.at[0, rows_of(k), columns(source)],
            dst_ref=opac.at[k, source],
            send_sem=a_send.at[k, i],
            recv_sem=a_recv.at[k, i],
            device_id=(source, t),
            device_id_type=MESH,
        )

    def send_colour(s):
        return pltpu.make_async_remote_copy(
            src_ref=colour.at[0, :, :, columns(2 * s + 1 - c)],
            dst_ref=cols.at[c, s],
            send_sem=c_send.at[s],
            recv_sem=c_recv.at[s],
            device_id=(sibling, t),
            device_id_type=MESH,
        )

    def recv_colour(s):
        return pltpu.make_async_remote_copy(
            src_ref=colour.at[0, :, :, columns(2 * s + 1 - c)],
            dst_ref=cols.at[1 - c, s],
            send_sem=c_send.at[s],
            recv_sem=c_recv.at[s],
            device_id=(sibling, t),
            device_id_type=MESH,
        )

    def send_remain(k, j):
        to = chip(sigma * j)
        return pltpu.make_async_remote_copy(
            src_ref=remain_out.at[k, to],
            dst_ref=remain_in.at[k, j],
            send_sem=r_send.at[k, j],
            recv_sem=r_recv.at[k, j],
            device_id=(2 * to + c, t),
            device_id_type=MESH,
        )

    def send_part(k, j):
        to = chip(-sigma) if j <= 4 else chip(sigma)
        return pltpu.make_async_remote_copy(
            src_ref=part_out.at[k, j],
            dst_ref=part_in.at[k, j - 1 if j <= 4 else j + 1],
            send_sem=p_send.at[k, j],
            recv_sem=p_recv.at[k, j - 1 if j <= 4 else j + 1],
            device_id=(2 * to + c, t),
            device_id_type=MESH,
        )

    def recv_part(k, slot):
        return pltpu.make_async_remote_copy(
            src_ref=part_out.at[k, 1],
            dst_ref=part_in.at[k, slot],
            send_sem=p_send.at[k, 1],
            recv_sem=p_recv.at[k, slot],
            device_id=(sibling, t),
            device_id_type=MESH,
        )

    def send_halo(k, side):
        middle = window.at[:, pl.ds(pl.multiple_of(height + k * chunk, chunk), chunk), :]
        at = 2 * height if side == 0 else 0
        return pltpu.make_async_remote_copy(
            src_ref=middle,
            dst_ref=window.at[:, pl.ds(pl.multiple_of(at + k * chunk, chunk), chunk), :],
            send_sem=h_send.at[k, side],
            recv_sem=h_recv.at[k, side],
            device_id=(d, above if side == 0 else below),
            device_id_type=MESH,
        )

    def send_beside(side):
        to = (d + GROUPS - 1) % GROUPS if side == 0 else (d + 1) % GROUPS
        source = HC if side == 0 else slab
        target = HC + slab if side == 0 else 0
        return pltpu.make_async_remote_copy(
            src_ref=vert.at[:, :, pl.ds(source, HC)],
            dst_ref=vert.at[:, :, pl.ds(target, HC)],
            send_sem=v_send.at[side],
            recv_sem=v_recv.at[side],
            device_id=(to, t),
            device_id_type=MESH,
        )

    def every(first, last, body):
        def outer(k, _):
            def inner(i, _):
                body(k, i)
                return 0

            return lax.fori_loop(first, last, inner, 0)

        lax.fori_loop(0, CHUNKS, outer, 0)

    every(1, GROUPS, lambda k, i: send_alpha(k, i).start())
    loop(CHIPS, lambda s: send_colour(s).start())

    flips = [(order[0] // (1 << bit)) % 2 for bit in range(4)]

    def in_front(bit, value, hidden):
        return jnp.where(flips[bit] == value, 1.0, hidden)

    def block_at(b):
        lanes = slab // LANES
        return (
            pl.multiple_of((b // lanes) * TILE_ROWS, TILE_ROWS),
            pl.multiple_of((b % lanes) * LANES, LANES),
        )

    def remains(k):
        own_alpha(k).wait()
        loop(GROUPS - 1, lambda i: recv_alpha(k, i + 1).wait_recv())

        def block(b):
            row, lane = block_at(b)
            place = (pl.ds(row, TILE_ROWS), pl.ds(lane, LANES))
            clear = [1.0 - opac[(k, g) + place].astype(F32) for g in range(GROUPS)]
            eight = [clear[g] * clear[g + 8] for g in range(8)]
            four = [eight[g] * eight[g + 4] for g in range(4)]
            two = [four[g] * four[g + 2] for g in range(2)]
            left = [in_front(0, g, two[1 - g]) for g in range(2)]
            left = [left[g % 2] * in_front(1, g // 2, four[g ^ 2]) for g in range(4)]
            left = [left[g % 4] * in_front(2, g // 4, eight[g ^ 4]) for g in range(8)]
            for g in range(GROUPS):
                value = left[g % 8] * in_front(3, g // 8, clear[g ^ 8])
                remain_out[(k, g // 2, g % 2) + place] = (value * value).astype(BF16)

        loop(blocks, block)
        loop(CHIPS - 1, lambda i: send_remain(k, i + 1).start())

    loop(CHUNKS, remains)

    loop(CHIPS, lambda s: own_colour(s).wait())
    loop(CHIPS, lambda s: recv_colour(s).wait_recv())

    def add_step(j):
        s = chip(-sigma * j)

        def of_chunk(k):
            send_remain(k, j).wait_recv()
            if j not in (4, 5):
                recv_part(k, j).wait_recv()

            def block(b):
                row, lane = block_at(b)
                place = (pl.ds(row, TILE_ROWS), pl.ds(lane, LANES))
                whole = (pl.ds(pl.multiple_of(k * chunk + row, TILE_ROWS), TILE_ROWS), pl.ds(lane, LANES))
                first = root(remain_in[(k, j, 0) + place])
                second = root(remain_in[(k, j, 1) + place])
                for channel in range(3):
                    total = first * cols[(0, s, channel) + whole].astype(F32)
                    total += second * cols[(1, s, channel) + whole].astype(F32)
                    if j not in (4, 5):
                        total += root(part_in[(k, j, channel) + place])
                    part_out[(k, j, channel) + place] = square(total)

            loop(blocks, block)
            send_part(k, j).start()

        loop(CHUNKS, of_chunk)

    for j in STEPS:
        add_step(j)

    def finish(k):
        recv_part(k, 0).wait_recv()
        recv_part(k, 8).wait_recv()

        def block(b):
            row, lane = block_at(b)
            place = (pl.ds(row, TILE_ROWS), pl.ds(lane, LANES))
            whole_row = pl.multiple_of(k * chunk + row, TILE_ROWS)
            whole = (pl.ds(whole_row, TILE_ROWS), pl.ds(lane, LANES))
            middle = (pl.ds(pl.multiple_of(height + whole_row, TILE_ROWS), TILE_ROWS), pl.ds(lane, LANES))
            first = root(remain_out[(k, y, 0) + place])
            second = root(remain_out[(k, y, 1) + place])
            for channel in range(3):
                total = first * cols[(0, y, channel) + whole].astype(F32)
                total += second * cols[(1, y, channel) + whole].astype(F32)
                total += root(part_in[(k, 0, channel) + place])
                total += root(part_in[(k, 8, channel) + place])
                high = total.astype(BF16)
                window[(channel,) + middle] = high
                low[(channel,) + whole] = (total - high.astype(F32)).astype(BF16)

        loop(blocks, block)
        send_halo(k, 0).start()
        send_halo(k, 1).start()

    loop(CHUNKS, finish)

    place = lax.broadcasted_iota(jnp.int32, (3 * height, height), 0)
    picks = jnp.zeros((3 * height, height), F32)
    for tap in range(4):
        taps = row_taps[tap, :][None, :]
        picks += jnp.where(taps == place, row_weights[tap, :].astype(F32)[None, :], 0.0)
    outside = ((place < height) & (t == 0)) | ((place >= 2 * height) & (t == tiles - 1))
    picks = jnp.transpose(jnp.where(outside, 0.0, picks)).astype(BF16)

    width = slab + 2 * HC
    p = t // bands_per_projector
    place = lax.broadcasted_iota(jnp.int32, (width, slab), 0) + (d * slab - HC)
    col_picks = jnp.zeros((width, slab), F32)
    for tap in range(4):
        taps = col_taps[p, tap, :][None, :]
        col_picks += jnp.where(taps == place, col_weights[p, tap, :].astype(F32)[None, :], 0.0)
    col_picks = col_picks.astype(BF16)

    def wait_halo(k):
        send_halo(k, 0).wait_recv()
        send_halo(k, 1).wait_recv()

    loop(CHUNKS, wait_halo)

    for channel in range(3):
        value = jnp.dot(picks, window[channel], preferred_element_type=F32)
        value += jnp.dot(picks[:, height : 2 * height], low[channel], preferred_element_type=F32)
        vert[channel, :, HC : HC + slab] = value.astype(BF16)
    send_beside(0).start()
    send_beside(1).start()

    within = (t % bands_per_projector) * height + lax.broadcasted_iota(jnp.int32, (height, slab), 0)
    within = within.astype(F32)
    proj_height = bands_per_projector * height
    ramp = jnp.minimum(
        1.0, jnp.minimum((within + 0.5) / BLEND, (proj_height - within - 0.5) / BLEND)
    )

    send_beside(0).wait_recv()
    send_beside(1).wait_recv()
    blended = [
        jnp.dot(vert[channel], col_picks, preferred_element_type=F32) * ramp for channel in range(3)
    ]
    for channel in range(3):
        mixed = matrix[p, channel, 0] * blended[0]
        mixed += matrix[p, channel, 1] * blended[1]
        mixed += matrix[p, channel, 2] * blended[2]
        out[channel] = mixed + offsets[p, channel]

    every(1, GROUPS, lambda k, i: send_alpha(k, i).wait_send())
    loop(CHIPS, lambda s: send_colour(s).wait_send())
    every(1, CHIPS, lambda k, j: send_remain(k, j).wait_send())
    for j in STEPS:
        loop(CHUNKS, lambda k: send_part(k, j).wait_send())
    loop(CHUNKS, lambda k: send_halo(k, 0).wait_send())
    loop(CHUNKS, lambda k: send_halo(k, 1).wait_send())
    send_beside(0).wait_send()
    send_beside(1).wait_send()


def shards(
    colour, alpha, depth_order, row_taps, row_weights, col_taps, col_weights, colour_matrix, offsets
):
    tiles = lax.axis_size("tile")
    height = colour.shape[2]
    slab = colour.shape[3] // GROUPS
    chunk = height // CHUNKS
    hbm = pl.BlockSpec(memory_space=pltpu.HBM)
    vmem = pl.BlockSpec(memory_space=pltpu.VMEM)
    smem = pl.BlockSpec(memory_space=pltpu.SMEM)
    dma = pltpu.SemaphoreType.DMA
    return pl.pallas_call(
        functools.partial(kernel, tiles // colour_matrix.shape[0], tiles),
        out_shape=jax.ShapeDtypeStruct((3, height, slab), F32),
        in_specs=[hbm, hbm, smem, vmem, vmem, vmem, vmem, smem, smem],
        out_specs=vmem,
        scratch_shapes=[
            pltpu.VMEM((CHUNKS, GROUPS, chunk, slab), BF16),
            pltpu.VMEM((2, CHIPS, 3, height, slab), BF16),
            pltpu.VMEM((CHUNKS, CHIPS, 2, chunk, slab), BF16),
            pltpu.VMEM((CHUNKS, CHIPS, 2, chunk, slab), BF16),
            pltpu.VMEM((CHUNKS, CHIPS, 3, chunk, slab), BF16),
            pltpu.VMEM((CHUNKS, CHIPS + 1, 3, chunk, slab), BF16),
            pltpu.VMEM((3, 3 * height, slab), BF16),
            pltpu.VMEM((3, height, slab), BF16),
            pltpu.VMEM((3, height, slab + 2 * HC), BF16),
            dma((CHUNKS, GROUPS)),
            dma((CHUNKS, GROUPS)),
            dma((CHUNKS,)),
            dma((CHIPS,)),
            dma((CHIPS,)),
            dma((CHIPS,)),
            dma((CHUNKS, CHIPS)),
            dma((CHUNKS, CHIPS)),
            dma((CHUNKS, CHIPS)),
            dma((CHUNKS, CHIPS + 1)),
            dma((CHUNKS, 2)),
            dma((CHUNKS, 2)),
            dma((2,)),
            dma((2,)),
        ],
        compiler_params=pltpu.CompilerParams(
            collective_id=0, has_side_effects=True, vmem_limit_bytes=48 * 2**20
        ),
    )(colour, alpha, depth_order, row_taps, row_weights, col_taps, col_weights, colour_matrix, offsets)


def solution(mesh):
    return jax.shard_map(
        shards,
        mesh=mesh,
        in_specs=(
            P("depth", None, "tile", None),
            P("depth", "tile", None),
            P(),
            P(None, "tile"),
            P(None, "tile"),
            P(None, None, "depth"),
            P(None, None, "depth"),
            P(),
            P(),
        ),
        out_specs=P(None, "tile", "depth"),
        check_vma=False,
    )
```

```python
import functools

import jax
import jax.numpy as jnp
from jax import lax
from jax.experimental import pallas as pl
from jax.experimental.pallas import tpu as pltpu
from jax.sharding import PartitionSpec as P

HC = 128
BLEND = 64
GROUPS = 16
CHIPS = 8
CHUNKS = 4
TILE_ROWS = 16
LANES = 128
STEPS = (4, 5, 3, 6, 2, 7, 1)
MESH = pl.DeviceIdType.MESH
F32 = jnp.float32
BF16 = jnp.bfloat16


def square(x):
    return (x * jnp.abs(x)).astype(BF16)


def root(v):
    v = v.astype(F32)
    return v * lax.rsqrt(jnp.maximum(jnp.abs(v), 1e-37))


def kernel(
    bands_per_projector,
    tiles,
    colour, alpha, order_in, row_taps_in, row_weights_in, col_taps_in, col_weights_in, matrix_in,
    offsets_in,
    out,
    order, row_taps, row_weights, col_taps, col_weights, matrix, offsets,
    opac, cols, remain_out, remain_in, part_out, part_in, window, low, vert,
    a_send, a_recv, a_own, c_own, c_send, c_recv, r_send, r_recv, p_send, p_recv,
    h_send, h_recv, v_send, v_recv, s_own,
):
    height, slab = out.shape[1], out.shape[2]
    chunk = height // CHUNKS
    blocks = (chunk // TILE_ROWS) * (slab // LANES)
    d = lax.axis_index("depth")
    t = lax.axis_index("tile")
    y, c = d // 2, d % 2
    sigma = 1 - 2 * c
    sibling = 2 * y + 1 - c
    below, above = (t + 1) % tiles, (t + tiles - 1) % tiles

    def chip(offset):
        return (y + offset + 2 * CHIPS) % CHIPS

    def columns(device):
        return pl.ds(pl.multiple_of(device * slab, slab), slab)

    def rows_of(k):
        return pl.ds(pl.multiple_of(k * chunk, chunk), chunk)

    barrier = pltpu.get_barrier_semaphore()

    def greet(i, _):
        pl.semaphore_signal(barrier, 1, device_id=((d + i) % GROUPS, t), device_id_type=MESH)
        return 0

    lax.fori_loop(1, GROUPS, greet, 0)
    pl.semaphore_signal(barrier, 1, device_id=(d, below), device_id_type=MESH)
    pl.semaphore_signal(barrier, 1, device_id=(d, above), device_id_type=MESH)

    def own_alpha(k):
        return pltpu.make_async_copy(
            alpha.at[0, rows_of(k), columns(d)], opac.at[k, d], a_own.at[k]
        )

    def own_colour(s):
        return pltpu.make_async_copy(
            colour.at[0, :, :, columns(2 * s + c)], cols.at[c, s], c_own.at[s]
        )

    def loop(n, body):
        def step(i, _):
            body(i)
            return 0

        lax.fori_loop(0, n, step, 0)

    small = [
        pltpu.make_async_copy(source, target, s_own.at[i])
        for i, (source, target) in enumerate((
            (order_in, order),
            (row_taps_in, row_taps),
            (row_weights_in, row_weights),
            (col_taps_in, col_taps),
            (col_weights_in, col_weights),
            (matrix_in, matrix),
            (offsets_in, offsets),
        ))
    ]
    for copy in small:
        copy.start()
    loop(CHUNKS, lambda k: own_alpha(k).start())
    loop(CHIPS, lambda s: own_colour(s).start())
    pl.semaphore_wait(barrier, GROUPS + 1)

    def send_alpha(k, i):
        to = (d + i) % GROUPS
        return pltpu.make_async_remote_copy(
            src_ref=alpha.at[0, rows_of(k), columns(to)],
            dst_ref=opac.at[k, d],
            send_sem=a_send.at[k, i],
            recv_sem=a_recv.at[k, i],
            device_id=(to, t),
            device_id_type=MESH,
        )

    def recv_alpha(k, i):
        source = (d + GROUPS - i) % GROUPS
        return pltpu.make_async_remote_copy(
            src_ref=alpha.at[0, rows_of(k), columns(source)],
            dst_ref=opac.at[k, source],
            send_sem=a_send.at[k, i],
            recv_sem=a_recv.at[k, i],
            device_id=(source, t),
            device_id_type=MESH,
        )

    def send_colour(s):
        return pltpu.make_async_remote_copy(
            src_ref=colour.at[0, :, :, columns(2 * s + 1 - c)],
            dst_ref=cols.at[c, s],
            send_sem=c_send.at[s],
            recv_sem=c_recv.at[s],
            device_id=(sibling, t),
            device_id_type=MESH,
        )

    def recv_colour(s):
        return pltpu.make_async_remote_copy(
            src_ref=colour.at[0, :, :, columns(2 * s + 1 - c)],
            dst_ref=cols.at[1 - c, s],
            send_sem=c_send.at[s],
            recv_sem=c_recv.at[s],
            device_id=(sibling, t),
            device_id_type=MESH,
        )

    def send_remain(k, j):
        to = chip(sigma * j)
        return pltpu.make_async_remote_copy(
            src_ref=remain_out.at[k, to],
            dst_ref=remain_in.at[k, j],
            send_sem=r_send.at[k, j],
            recv_sem=r_recv.at[k, j],
            device_id=(2 * to + c, t),
            device_id_type=MESH,
        )

    def send_part(k, j):
        to = chip(-sigma) if j <= 4 else chip(sigma)
        return pltpu.make_async_remote_copy(
            src_ref=part_out.at[k, j],
            dst_ref=part_in.at[k, j - 1 if j <= 4 else j + 1],
            send_sem=p_send.at[k, j],
            recv_sem=p_recv.at[k, j - 1 if j <= 4 else j + 1],
            device_id=(2 * to + c, t),
            device_id_type=MESH,
        )

    def recv_part(k, slot):
        return pltpu.make_async_remote_copy(
            src_ref=part_out.at[k, 1],
            dst_ref=part_in.at[k, slot],
            send_sem=p_send.at[k, 1],
            recv_sem=p_recv.at[k, slot],
            device_id=(sibling, t),
            device_id_type=MESH,
        )

    def send_halo(k, side):
        middle = window.at[:, pl.ds(pl.multiple_of(height + k * chunk, chunk), chunk), :]
        at = 2 * height if side == 0 else 0
        return pltpu.make_async_remote_copy(
            src_ref=middle,
            dst_ref=window.at[:, pl.ds(pl.multiple_of(at + k * chunk, chunk), chunk), :],
            send_sem=h_send.at[k, side],
            recv_sem=h_recv.at[k, side],
            device_id=(d, above if side == 0 else below),
            device_id_type=MESH,
        )

    def send_beside(side):
        to = (d + GROUPS - 1) % GROUPS if side == 0 else (d + 1) % GROUPS
        source = HC if side == 0 else slab
        target = HC + slab if side == 0 else 0
        return pltpu.make_async_remote_copy(
            src_ref=vert.at[:, :, pl.ds(source, HC)],
            dst_ref=vert.at[:, :, pl.ds(target, HC)],
            send_sem=v_send.at[side],
            recv_sem=v_recv.at[side],
            device_id=(to, t),
            device_id_type=MESH,
        )

    def every(first, last, body):
        def outer(k, _):
            def inner(i, _):
                body(k, i)
                return 0

            return lax.fori_loop(first, last, inner, 0)

        lax.fori_loop(0, CHUNKS, outer, 0)

    every(1, GROUPS, lambda k, i: send_alpha(k, i).start())
    loop(CHIPS, lambda s: send_colour(s).start())

    for copy in small:
        copy.wait()
    flips = [(order[0] // (1 << bit)) % 2 for bit in range(4)]

    def in_front(bit, value, hidden):
        return jnp.where(flips[bit] == value, 1.0, hidden)

    def block_at(b):
        lanes = slab // LANES
        return (
            pl.multiple_of((b // lanes) * TILE_ROWS, TILE_ROWS),
            pl.multiple_of((b % lanes) * LANES, LANES),
        )

    def remains(k):
        own_alpha(k).wait()
        loop(GROUPS - 1, lambda i: recv_alpha(k, i + 1).wait_recv())

        def block(b):
            row, lane = block_at(b)
            place = (pl.ds(row, TILE_ROWS), pl.ds(lane, LANES))
            clear = [1.0 - opac[(k, g) + place].astype(F32) for g in range(GROUPS)]
            eight = [clear[g] * clear[g + 8] for g in range(8)]
            four = [eight[g] * eight[g + 4] for g in range(4)]
            two = [four[g] * four[g + 2] for g in range(2)]
            left = [in_front(0, g, two[1 - g]) for g in range(2)]
            left = [left[g % 2] * in_front(1, g // 2, four[g ^ 2]) for g in range(4)]
            left = [left[g % 4] * in_front(2, g // 4, eight[g ^ 4]) for g in range(8)]
            for g in range(GROUPS):
                value = left[g % 8] * in_front(3, g // 8, clear[g ^ 8])
                remain_out[(k, g // 2, g % 2) + place] = (value * value).astype(BF16)

        loop(blocks, block)
        loop(CHIPS - 1, lambda i: send_remain(k, i + 1).start())

    loop(CHUNKS, remains)

    loop(CHIPS, lambda s: own_colour(s).wait())
    loop(CHIPS, lambda s: recv_colour(s).wait_recv())

    def add_step(j):
        s = chip(-sigma * j)

        def of_chunk(k):
            send_remain(k, j).wait_recv()
            if j not in (4, 5):
                recv_part(k, j).wait_recv()

            def block(b):
                row, lane = block_at(b)
                place = (pl.ds(row, TILE_ROWS), pl.ds(lane, LANES))
                whole = (pl.ds(pl.multiple_of(k * chunk + row, TILE_ROWS), TILE_ROWS), pl.ds(lane, LANES))
                first = root(remain_in[(k, j, 0) + place])
                second = root(remain_in[(k, j, 1) + place])
                for channel in range(3):
                    total = first * cols[(0, s, channel) + whole].astype(F32)
                    total += second * cols[(1, s, channel) + whole].astype(F32)
                    if j not in (4, 5):
                        total += root(part_in[(k, j, channel) + place])
                    part_out[(k, j, channel) + place] = square(total)

            loop(blocks, block)
            send_part(k, j).start()

        loop(CHUNKS, of_chunk)

    for j in STEPS:
        add_step(j)

    def finish(k):
        recv_part(k, 0).wait_recv()
        recv_part(k, 8).wait_recv()

        def block(b):
            row, lane = block_at(b)
            place = (pl.ds(row, TILE_ROWS), pl.ds(lane, LANES))
            whole_row = pl.multiple_of(k * chunk + row, TILE_ROWS)
            whole = (pl.ds(whole_row, TILE_ROWS), pl.ds(lane, LANES))
            middle = (pl.ds(pl.multiple_of(height + whole_row, TILE_ROWS), TILE_ROWS), pl.ds(lane, LANES))
            first = root(remain_out[(k, y, 0) + place])
            second = root(remain_out[(k, y, 1) + place])
            for channel in range(3):
                total = first * cols[(0, y, channel) + whole].astype(F32)
                total += second * cols[(1, y, channel) + whole].astype(F32)
                total += root(part_in[(k, 0, channel) + place])
                total += root(part_in[(k, 8, channel) + place])
                high = total.astype(BF16)
                window[(channel,) + middle] = high
                low[(channel,) + whole] = (total - high.astype(F32)).astype(BF16)

        loop(blocks, block)
        send_halo(k, 0).start()
        send_halo(k, 1).start()

    loop(CHUNKS, finish)

    place = lax.broadcasted_iota(jnp.int32, (3 * height, height), 0)
    picks = jnp.zeros((3 * height, height), F32)
    for tap in range(4):
        taps = row_taps[tap, :][None, :]
        picks += jnp.where(taps == place, row_weights[tap, :].astype(F32)[None, :], 0.0)
    outside = ((place < height) & (t == 0)) | ((place >= 2 * height) & (t == tiles - 1))
    picks = jnp.transpose(jnp.where(outside, 0.0, picks)).astype(BF16)

    width = slab + 2 * HC
    p = t // bands_per_projector
    place = lax.broadcasted_iota(jnp.int32, (width, slab), 0) + (d * slab - HC)
    col_picks = jnp.zeros((width, slab), F32)
    for tap in range(4):
        taps = col_taps[p, tap, :][None, :]
        col_picks += jnp.where(taps == place, col_weights[p, tap, :].astype(F32)[None, :], 0.0)
    col_picks = col_picks.astype(BF16)

    def wait_halo(k):
        send_halo(k, 0).wait_recv()
        send_halo(k, 1).wait_recv()

    loop(CHUNKS, wait_halo)

    for channel in range(3):
        value = jnp.dot(picks, window[channel], preferred_element_type=F32)
        value += jnp.dot(picks[:, height : 2 * height], low[channel], preferred_element_type=F32)
        vert[channel, :, HC : HC + slab] = value.astype(BF16)
    send_beside(0).start()
    send_beside(1).start()

    within = (t % bands_per_projector) * height + lax.broadcasted_iota(jnp.int32, (height, slab), 0)
    within = within.astype(F32)
    proj_height = bands_per_projector * height
    ramp = jnp.minimum(
        1.0, jnp.minimum((within + 0.5) / BLEND, (proj_height - within - 0.5) / BLEND)
    )

    send_beside(0).wait_recv()
    send_beside(1).wait_recv()
    blended = [
        jnp.dot(vert[channel], col_picks, preferred_element_type=F32) * ramp for channel in range(3)
    ]
    for channel in range(3):
        mixed = matrix[channel, p, 0] * blended[0]
        mixed += matrix[channel, p, 1] * blended[1]
        mixed += matrix[channel, p, 2] * blended[2]
        out[channel] = mixed + offsets[p, channel]

    every(1, GROUPS, lambda k, i: send_alpha(k, i).wait_send())
    loop(CHIPS, lambda s: send_colour(s).wait_send())
    every(1, CHIPS, lambda k, j: send_remain(k, j).wait_send())
    for j in STEPS:
        loop(CHUNKS, lambda k: send_part(k, j).wait_send())
    loop(CHUNKS, lambda k: send_halo(k, 0).wait_send())
    loop(CHUNKS, lambda k: send_halo(k, 1).wait_send())
    send_beside(0).wait_send()
    send_beside(1).wait_send()


def shards(
    colour, alpha, depth_order, row_taps, row_weights, col_taps, col_weights, colour_matrix, offsets
):
    tiles = lax.axis_size("tile")
    height = colour.shape[2]
    slab = colour.shape[3] // GROUPS
    chunk = height // CHUNKS
    hbm = pl.BlockSpec(memory_space=pltpu.HBM)
    vmem = pl.BlockSpec(memory_space=pltpu.VMEM)
    matrix = jnp.transpose(colour_matrix, (1, 0, 2))
    dma = pltpu.SemaphoreType.DMA
    return pl.pallas_call(
        functools.partial(kernel, tiles // colour_matrix.shape[0], tiles),
        out_shape=jax.ShapeDtypeStruct((3, height, slab), F32),
        in_specs=[hbm] * 9,
        out_specs=vmem,
        scratch_shapes=[
            pltpu.SMEM(depth_order.shape, depth_order.dtype),
            pltpu.VMEM(row_taps.shape, row_taps.dtype),
            pltpu.VMEM(row_weights.shape, row_weights.dtype),
            pltpu.VMEM(col_taps.shape, col_taps.dtype),
            pltpu.VMEM(col_weights.shape, col_weights.dtype),
            pltpu.SMEM(matrix.shape, matrix.dtype),
            pltpu.SMEM(offsets.shape, offsets.dtype),
            pltpu.VMEM((CHUNKS, GROUPS, chunk, slab), BF16),
            pltpu.VMEM((2, CHIPS, 3, height, slab), BF16),
            pltpu.VMEM((CHUNKS, CHIPS, 2, chunk, slab), BF16),
            pltpu.VMEM((CHUNKS, CHIPS, 2, chunk, slab), BF16),
            pltpu.VMEM((CHUNKS, CHIPS, 3, chunk, slab), BF16),
            pltpu.VMEM((CHUNKS, CHIPS + 1, 3, chunk, slab), BF16),
            pltpu.VMEM((3, 3 * height, slab), BF16),
            pltpu.VMEM((3, height, slab), BF16),
            pltpu.VMEM((3, height, slab + 2 * HC), BF16),
            dma((CHUNKS, GROUPS)),
            dma((CHUNKS, GROUPS)),
            dma((CHUNKS,)),
            dma((CHIPS,)),
            dma((CHIPS,)),
            dma((CHIPS,)),
            dma((CHUNKS, CHIPS)),
            dma((CHUNKS, CHIPS)),
            dma((CHUNKS, CHIPS)),
            dma((CHUNKS, CHIPS + 1)),
            dma((CHUNKS, 2)),
            dma((CHUNKS, 2)),
            dma((2,)),
            dma((2,)),
            dma((7,)),
        ],
        compiler_params=pltpu.CompilerParams(
            collective_id=0, has_side_effects=True, vmem_limit_bytes=63 * 2**20
        ),
    )(colour, alpha, depth_order, row_taps, row_weights, col_taps, col_weights, matrix, offsets)


def solution(mesh):
    return jax.shard_map(
        shards,
        mesh=mesh,
        in_specs=(
            P("depth", None, "tile", None),
            P("depth", "tile", None),
            P(),
            P(None, "tile"),
            P(None, "tile"),
            P(None, None, "depth"),
            P(None, None, "depth"),
            P(),
            P(),
        ),
        out_specs=P(None, "tile", "depth"),
        check_vma=False,
    )
```

```python
import functools

import jax
import jax.numpy as jnp
from jax import lax
from jax.experimental import pallas as pl
from jax.experimental.pallas import tpu as pltpu
from jax.sharding import PartitionSpec as P

HC = 128
BLEND = 64
GROUPS = 16
CHIPS = 8
CHUNKS = 4
TILE_ROWS = 16
LANES = 128
STEPS = (4, 5, 3, 6, 2, 7, 1)
MESH = pl.DeviceIdType.MESH
F32 = jnp.float32
BF16 = jnp.bfloat16


def square(x):
    return (x * jnp.abs(x)).astype(BF16)


def root(v):
    v = v.astype(F32)
    return v * lax.rsqrt(jnp.maximum(jnp.abs(v), 1e-37))


def kernel(
    bands_per_projector,
    tiles,
    colour, alpha, order_in, row_taps_in, row_weights_in, col_taps_in, col_weights_in, matrix_in,
    offsets_in,
    out,
    order, row_taps, row_weights, col_taps, col_weights, matrix, offsets,
    opac, cols, left_all, kept, remain_out, remain_in, part_out, part_in, window, low, vert, row_picks, col_matrix,
    a_send, a_recv, a_own, c_own, c_send, c_recv, r_send, r_recv, p_send, p_recv,
    h_send, h_recv, v_send, v_recv, s_own,
):
    height, slab = out.shape[1], out.shape[2]
    chunk = height // CHUNKS
    blocks = (chunk // TILE_ROWS) * (slab // LANES)
    d = lax.axis_index("depth")
    t = lax.axis_index("tile")
    y, c = d // 2, d % 2
    sigma = 1 - 2 * c
    sibling = 2 * y + 1 - c
    below, above = (t + 1) % tiles, (t + tiles - 1) % tiles

    def chip(offset):
        return (y + offset + 2 * CHIPS) % CHIPS

    def columns(device):
        return pl.ds(pl.multiple_of(device * slab, slab), slab)

    def rows_of(k):
        return pl.ds(pl.multiple_of(k * chunk, chunk), chunk)

    barrier = pltpu.get_barrier_semaphore()

    def greet(i, _):
        pl.semaphore_signal(barrier, 1, device_id=((d + i) % GROUPS, t), device_id_type=MESH)
        return 0

    lax.fori_loop(1, GROUPS, greet, 0)
    pl.semaphore_signal(barrier, 1, device_id=(d, below), device_id_type=MESH)
    pl.semaphore_signal(barrier, 1, device_id=(d, above), device_id_type=MESH)

    def own_alpha(k):
        return pltpu.make_async_copy(
            alpha.at[0, rows_of(k), columns(d)], opac.at[k, d], a_own.at[k]
        )

    def own_colour(s):
        return pltpu.make_async_copy(
            colour.at[0, :, :, columns(2 * s + c)], cols.at[c, s], c_own.at[s]
        )

    def loop(n, body):
        def step(i, _):
            body(i)
            return 0

        lax.fori_loop(0, n, step, 0)

    small = [
        pltpu.make_async_copy(source, target, s_own.at[i])
        for i, (source, target) in enumerate((
            (order_in, order),
            (row_taps_in, row_taps),
            (row_weights_in, row_weights),
            (col_taps_in, col_taps),
            (col_weights_in, col_weights),
            (matrix_in, matrix),
            (offsets_in, offsets),
        ))
    ]
    for copy in small:
        copy.start()
    loop(CHUNKS, lambda k: own_alpha(k).start())
    loop(CHIPS, lambda s: own_colour(s).start())
    pl.semaphore_wait(barrier, GROUPS + 1)

    def send_alpha(k, i):
        to = (d + i) % GROUPS
        return pltpu.make_async_remote_copy(
            src_ref=alpha.at[0, rows_of(k), columns(to)],
            dst_ref=opac.at[k, d],
            send_sem=a_send.at[k, i],
            recv_sem=a_recv.at[k, i],
            device_id=(to, t),
            device_id_type=MESH,
        )

    def recv_alpha(k, i):
        source = (d + GROUPS - i) % GROUPS
        return pltpu.make_async_remote_copy(
            src_ref=alpha.at[0, rows_of(k), columns(source)],
            dst_ref=opac.at[k, source],
            send_sem=a_send.at[k, i],
            recv_sem=a_recv.at[k, i],
            device_id=(source, t),
            device_id_type=MESH,
        )

    def send_colour(s):
        return pltpu.make_async_remote_copy(
            src_ref=colour.at[0, :, :, columns(2 * s + 1 - c)],
            dst_ref=cols.at[c, s],
            send_sem=c_send.at[s],
            recv_sem=c_recv.at[s],
            device_id=(sibling, t),
            device_id_type=MESH,
        )

    def recv_colour(s):
        return pltpu.make_async_remote_copy(
            src_ref=colour.at[0, :, :, columns(2 * s + 1 - c)],
            dst_ref=cols.at[1 - c, s],
            send_sem=c_send.at[s],
            recv_sem=c_recv.at[s],
            device_id=(sibling, t),
            device_id_type=MESH,
        )

    def send_remain(k, j):
        to = chip(sigma * j)
        first = 1 if j in (4, 5) else 0
        return pltpu.make_async_remote_copy(
            src_ref=remain_out.at[k, j, pl.ds(first, 2 - first)],
            dst_ref=remain_in.at[k, j, pl.ds(first, 2 - first)],
            send_sem=r_send.at[k, j],
            recv_sem=r_recv.at[k, j],
            device_id=(2 * to + c, t),
            device_id_type=MESH,
        )

    def send_part(k, j):
        to = chip(-sigma) if j <= 4 else chip(sigma)
        return pltpu.make_async_remote_copy(
            src_ref=part_out.at[k, j],
            dst_ref=part_in.at[k, j - 1 if j <= 4 else j + 1],
            send_sem=p_send.at[k, j],
            recv_sem=p_recv.at[k, j - 1 if j <= 4 else j + 1],
            device_id=(2 * to + c, t),
            device_id_type=MESH,
        )

    def recv_part(k, slot):
        return pltpu.make_async_remote_copy(
            src_ref=part_out.at[k, 1],
            dst_ref=part_in.at[k, slot],
            send_sem=p_send.at[k, 1],
            recv_sem=p_recv.at[k, slot],
            device_id=(sibling, t),
            device_id_type=MESH,
        )

    def send_halo(k, side):
        middle = window.at[:, pl.ds(pl.multiple_of(height + k * chunk, chunk), chunk), :]
        at = 2 * height if side == 0 else 0
        return pltpu.make_async_remote_copy(
            src_ref=middle,
            dst_ref=window.at[:, pl.ds(pl.multiple_of(at + k * chunk, chunk), chunk), :],
            send_sem=h_send.at[k, side],
            recv_sem=h_recv.at[k, side],
            device_id=(d, above if side == 0 else below),
            device_id_type=MESH,
        )

    def send_beside(side):
        to = (d + GROUPS - 1) % GROUPS if side == 0 else (d + 1) % GROUPS
        source = HC if side == 0 else slab
        target = HC + slab if side == 0 else 0
        return pltpu.make_async_remote_copy(
            src_ref=vert.at[:, :, pl.ds(source, HC)],
            dst_ref=vert.at[:, :, pl.ds(target, HC)],
            send_sem=v_send.at[side],
            recv_sem=v_recv.at[side],
            device_id=(to, t),
            device_id_type=MESH,
        )

    def every(first, last, body):
        def outer(k, _):
            def inner(i, _):
                body(k, i)
                return 0

            return lax.fori_loop(first, last, inner, 0)

        lax.fori_loop(0, CHUNKS, outer, 0)

    every(1, GROUPS, lambda k, i: send_alpha(k, i).start())
    loop(CHIPS, lambda s: send_colour(s).start())

    for copy in small:
        copy.wait()
    flips = [(order[0] // (1 << bit)) % 2 for bit in range(4)]

    place = lax.broadcasted_iota(jnp.int32, (3 * height, height), 0)
    picks = jnp.zeros((3 * height, height), F32)
    for tap in range(4):
        taps = row_taps[tap, :][None, :]
        picks += jnp.where(taps == place, row_weights[tap, :].astype(F32)[None, :], 0.0)
    outside = ((place < height) & (t == 0)) | ((place >= 2 * height) & (t == tiles - 1))
    row_picks[...] = jnp.transpose(jnp.where(outside, 0.0, picks)).astype(BF16)

    width = slab + 2 * HC
    p = t // bands_per_projector
    place = lax.broadcasted_iota(jnp.int32, (width, slab), 0) + (d * slab - HC)
    col_picks = jnp.zeros((width, slab), F32)
    for tap in range(4):
        taps = col_taps[p, tap, :][None, :]
        col_picks += jnp.where(taps == place, col_weights[p, tap, :].astype(F32)[None, :], 0.0)
    col_matrix[...] = col_picks.astype(BF16)


    def in_front(bit, value, hidden):
        return jnp.where(flips[bit] == value, 1.0, hidden)

    def block_at(b):
        lanes = slab // LANES
        return (
            pl.multiple_of((b // lanes) * TILE_ROWS, TILE_ROWS),
            pl.multiple_of((b % lanes) * LANES, LANES),
        )

    def remains(k):
        own_alpha(k).wait()
        loop(GROUPS - 1, lambda i: recv_alpha(k, i + 1).wait_recv())

        def block(b):
            row, lane = block_at(b)
            place = (pl.ds(row, TILE_ROWS), pl.ds(lane, LANES))
            clear = [1.0 - opac[(k, g) + place].astype(F32) for g in range(GROUPS)]
            eight = [clear[g] * clear[g + 8] for g in range(8)]
            four = [eight[g] * eight[g + 4] for g in range(4)]
            two = [four[g] * four[g + 2] for g in range(2)]
            left = [in_front(0, g, two[1 - g]) for g in range(2)]
            left = [left[g % 2] * in_front(1, g // 2, four[g ^ 2]) for g in range(4)]
            left = [left[g % 4] * in_front(2, g // 4, eight[g ^ 4]) for g in range(8)]
            for g in range(GROUPS):
                left_all[g] = left[g % 8] * in_front(3, g // 8, clear[g ^ 8])
            kept[(k, 0) + place] = left_all[2 * y]
            kept[(k, 1) + place] = left_all[2 * y + 1]
            for j, ends in (((4, 3, 2, 1), 2), ((5, 6, 7), 3)):
                scale = left_all[2 * chip(sigma * j[0])]
                kept[(k, ends) + place] = scale
                scale = 1.0 / scale
                for i in j:
                    for core in range(2):
                        if i != j[0] or core:
                            value = left_all[2 * chip(sigma * i) + core] * scale
                            remain_out[(k, i, core) + place] = (value * value).astype(BF16)

        loop(blocks, block)
        for j in STEPS:
            send_remain(k, j).start()

    loop(CHUNKS, remains)

    loop(CHIPS, lambda s: own_colour(s).wait())
    loop(CHIPS, lambda s: recv_colour(s).wait_recv())
    loop(CHIPS, lambda s: send_colour(s).wait_send())
    every(1, GROUPS, lambda k, i: send_alpha(k, i).wait_send())

    def add_step(j):
        s = chip(-sigma * j)

        def of_chunk(k):
            send_remain(k, j).wait_recv()
            if j not in (4, 5):
                recv_part(k, j).wait_recv()

            def block(b):
                row, lane = block_at(b)
                place = (pl.ds(row, TILE_ROWS), pl.ds(lane, LANES))
                whole = (pl.ds(pl.multiple_of(k * chunk + row, TILE_ROWS), TILE_ROWS), pl.ds(lane, LANES))
                if j not in (4, 5):
                    first = root(remain_in[(k, j, 0) + place])
                second = root(remain_in[(k, j, 1) + place])
                for channel in range(3):
                    total = cols[(0, s, channel) + whole].astype(F32)
                    if j not in (4, 5):
                        total = first * total
                    total += second * cols[(1, s, channel) + whole].astype(F32)
                    if j not in (4, 5):
                        total += root(part_in[(k, j, channel) + place])
                    part_out[(k, j, channel) + place] = square(total)

            loop(blocks, block)
            send_part(k, j).start()

        loop(CHUNKS, of_chunk)

    for j in STEPS:
        add_step(j)

    def finish(k):
        recv_part(k, 0).wait_recv()
        recv_part(k, 8).wait_recv()

        def block(b):
            row, lane = block_at(b)
            place = (pl.ds(row, TILE_ROWS), pl.ds(lane, LANES))
            whole_row = pl.multiple_of(k * chunk + row, TILE_ROWS)
            whole = (pl.ds(whole_row, TILE_ROWS), pl.ds(lane, LANES))
            middle = (pl.ds(pl.multiple_of(height + whole_row, TILE_ROWS), TILE_ROWS), pl.ds(lane, LANES))
            first, second = kept[(k, 0) + place], kept[(k, 1) + place]
            far, near = kept[(k, 2) + place], kept[(k, 3) + place]
            for channel in range(3):
                total = first * cols[(0, y, channel) + whole].astype(F32)
                total += second * cols[(1, y, channel) + whole].astype(F32)
                total += far * root(part_in[(k, 0, channel) + place])
                total += near * root(part_in[(k, 8, channel) + place])
                high = total.astype(BF16)
                window[(channel,) + middle] = high
                low[(channel,) + whole] = (total - high.astype(F32)).astype(BF16)

        loop(blocks, block)
        send_halo(k, 0).start()
        send_halo(k, 1).start()

    loop(CHUNKS, finish)

    for j in STEPS:
        loop(CHUNKS, lambda k: send_remain(k, j).wait_send())
        loop(CHUNKS, lambda k: send_part(k, j).wait_send())

    def wait_halo(k):
        send_halo(k, 0).wait_recv()
        send_halo(k, 1).wait_recv()

    loop(CHUNKS, wait_halo)

    for channel in range(3):
        value = jnp.dot(row_picks[...], window[channel], preferred_element_type=F32)
        value += jnp.dot(row_picks[:, height : 2 * height], low[channel], preferred_element_type=F32)
        vert[channel, :, HC : HC + slab] = value.astype(BF16)
    send_beside(0).start()
    send_beside(1).start()

    within = (t % bands_per_projector) * height + lax.broadcasted_iota(jnp.int32, (height, slab), 0)
    within = within.astype(F32)
    proj_height = bands_per_projector * height
    ramp = jnp.minimum(
        1.0, jnp.minimum((within + 0.5) / BLEND, (proj_height - within - 0.5) / BLEND)
    )

    send_beside(0).wait_recv()
    send_beside(1).wait_recv()
    blended = [
        jnp.dot(vert[channel], col_matrix[...], preferred_element_type=F32) * ramp for channel in range(3)
    ]
    for channel in range(3):
        mixed = matrix[channel, p, 0] * blended[0]
        mixed += matrix[channel, p, 1] * blended[1]
        mixed += matrix[channel, p, 2] * blended[2]
        out[channel] = mixed + offsets[p, channel]

    loop(CHUNKS, lambda k: send_halo(k, 0).wait_send())
    loop(CHUNKS, lambda k: send_halo(k, 1).wait_send())
    send_beside(0).wait_send()
    send_beside(1).wait_send()


def shards(
    colour, alpha, depth_order, row_taps, row_weights, col_taps, col_weights, colour_matrix, offsets
):
    tiles = lax.axis_size("tile")
    height = colour.shape[2]
    slab = colour.shape[3] // GROUPS
    chunk = height // CHUNKS
    hbm = pl.BlockSpec(memory_space=pltpu.HBM)
    vmem = pl.BlockSpec(memory_space=pltpu.VMEM)
    matrix = jnp.transpose(colour_matrix, (1, 0, 2))
    dma = pltpu.SemaphoreType.DMA
    return pl.pallas_call(
        functools.partial(kernel, tiles // colour_matrix.shape[0], tiles),
        out_shape=jax.ShapeDtypeStruct((3, height, slab), F32),
        in_specs=[hbm] * 9,
        out_specs=vmem,
        scratch_shapes=[
            pltpu.SMEM(depth_order.shape, depth_order.dtype),
            pltpu.VMEM(row_taps.shape, row_taps.dtype),
            pltpu.VMEM(row_weights.shape, row_weights.dtype),
            pltpu.VMEM(col_taps.shape, col_taps.dtype),
            pltpu.VMEM(col_weights.shape, col_weights.dtype),
            pltpu.SMEM(matrix.shape, matrix.dtype),
            pltpu.SMEM(offsets.shape, offsets.dtype),
            pltpu.VMEM((CHUNKS, GROUPS, chunk, slab), BF16),
            pltpu.VMEM((2, CHIPS, 3, height, slab), BF16),
            pltpu.VMEM((GROUPS, TILE_ROWS, LANES), F32),
            pltpu.VMEM((CHUNKS, 4, chunk, slab), F32),
            pltpu.VMEM((CHUNKS, CHIPS, 2, chunk, slab), BF16),
            pltpu.VMEM((CHUNKS, CHIPS, 2, chunk, slab), BF16),
            pltpu.VMEM((CHUNKS, CHIPS, 3, chunk, slab), BF16),
            pltpu.VMEM((CHUNKS, CHIPS + 1, 3, chunk, slab), BF16),
            pltpu.VMEM((3, 3 * height, slab), BF16),
            pltpu.VMEM((3, height, slab), BF16),
            pltpu.VMEM((3, height, slab + 2 * HC), BF16),
            pltpu.VMEM((height, 3 * height), BF16),
            pltpu.VMEM((slab + 2 * HC, slab), BF16),
            dma((CHUNKS, GROUPS)),
            dma((CHUNKS, GROUPS)),
            dma((CHUNKS,)),
            dma((CHIPS,)),
            dma((CHIPS,)),
            dma((CHIPS,)),
            dma((CHUNKS, CHIPS)),
            dma((CHUNKS, CHIPS)),
            dma((CHUNKS, CHIPS)),
            dma((CHUNKS, CHIPS + 1)),
            dma((CHUNKS, 2)),
            dma((CHUNKS, 2)),
            dma((2,)),
            dma((2,)),
            dma((7,)),
        ],
        compiler_params=pltpu.CompilerParams(
            collective_id=0, has_side_effects=True, vmem_limit_bytes=63 * 2**20
        ),
    )(colour, alpha, depth_order, row_taps, row_weights, col_taps, col_weights, matrix, offsets)


def solution(mesh):
    return jax.shard_map(
        shards,
        mesh=mesh,
        in_specs=(
            P("depth", None, "tile", None),
            P("depth", "tile", None),
            P(),
            P(None, "tile"),
            P(None, "tile"),
            P(None, None, "depth"),
            P(None, None, "depth"),
            P(),
            P(),
        ),
        out_specs=P(None, "tile", "depth"),
        check_vma=False,
    )
```

```python
import functools

import jax
import jax.numpy as jnp
from jax import lax
from jax.experimental import pallas as pl
from jax.experimental.pallas import tpu as pltpu
from jax.sharding import PartitionSpec as P

HC = 128
BLEND = 64
GROUPS = 16
CHIPS = 8
CHUNKS = 4
TILE_ROWS = 16
LANES = 128
STEPS = (4, 5, 3, 6, 2, 7, 1)
MESH = pl.DeviceIdType.MESH
F32 = jnp.float32
BF16 = jnp.bfloat16


def square(x):
    return (x * jnp.abs(x)).astype(BF16)


def root(v):
    v = v.astype(F32)
    return v * lax.rsqrt(jnp.maximum(jnp.abs(v), 1e-37))


def kernel(
    bands_per_projector,
    tiles,
    colour, alpha, order_in, row_taps_in, row_weights_in, col_taps_in, col_weights_in, matrix_in,
    offsets_in,
    out,
    order, row_taps, row_weights, col_taps, col_weights, matrix, offsets,
    opac, cols, left_all, kept, remain_out, remain_in, part_out, part_in, window, low, vert,
    row_picks, col_matrix, partial,
    a_send, a_recv, a_own, c_own, c_send, c_recv, r_send, r_recv, p_send, p_recv,
    h_send, h_recv, v_send, v_recv, s_own,
):
    height, slab = out.shape[1], out.shape[2]
    chunk = height // CHUNKS
    blocks = (chunk // TILE_ROWS) * (slab // LANES)
    d = lax.axis_index("depth")
    t = lax.axis_index("tile")
    y, c = d // 2, d % 2
    sigma = 1 - 2 * c
    sibling = 2 * y + 1 - c
    below, above = (t + 1) % tiles, (t + tiles - 1) % tiles

    def chip(offset):
        return (y + offset + 2 * CHIPS) % CHIPS

    def columns(device):
        return pl.ds(pl.multiple_of(device * slab, slab), slab)

    def rows_of(k):
        return pl.ds(pl.multiple_of(k * chunk, chunk), chunk)

    barrier = pltpu.get_barrier_semaphore()

    def greet(i, _):
        pl.semaphore_signal(barrier, 1, device_id=((d + i) % GROUPS, t), device_id_type=MESH)
        return 0

    lax.fori_loop(1, GROUPS, greet, 0)
    pl.semaphore_signal(barrier, 1, device_id=(d, below), device_id_type=MESH)
    pl.semaphore_signal(barrier, 1, device_id=(d, above), device_id_type=MESH)

    def own_alpha(k):
        return pltpu.make_async_copy(
            alpha.at[0, rows_of(k), columns(d)], opac.at[k, d], a_own.at[k]
        )

    def own_colour(s):
        return pltpu.make_async_copy(
            colour.at[0, :, :, columns(2 * s + c)], cols.at[c, s], c_own.at[s]
        )

    def loop(n, body):
        def step(i, _):
            body(i)
            return 0

        lax.fori_loop(0, n, step, 0)

    small = [
        pltpu.make_async_copy(source, target, s_own.at[i])
        for i, (source, target) in enumerate((
            (order_in, order),
            (row_taps_in, row_taps),
            (row_weights_in, row_weights),
            (col_taps_in, col_taps),
            (col_weights_in, col_weights),
            (matrix_in, matrix),
            (offsets_in, offsets),
        ))
    ]
    for copy in small:
        copy.start()
    loop(CHUNKS, lambda k: own_alpha(k).start())
    loop(CHIPS, lambda s: own_colour(s).start())
    pl.semaphore_wait(barrier, GROUPS + 1)

    def send_alpha(k, i):
        to = (d + i) % GROUPS
        return pltpu.make_async_remote_copy(
            src_ref=alpha.at[0, rows_of(k), columns(to)],
            dst_ref=opac.at[k, d],
            send_sem=a_send.at[k, i],
            recv_sem=a_recv.at[k, i],
            device_id=(to, t),
            device_id_type=MESH,
        )

    def recv_alpha(k, i):
        source = (d + GROUPS - i) % GROUPS
        return pltpu.make_async_remote_copy(
            src_ref=alpha.at[0, rows_of(k), columns(source)],
            dst_ref=opac.at[k, source],
            send_sem=a_send.at[k, i],
            recv_sem=a_recv.at[k, i],
            device_id=(source, t),
            device_id_type=MESH,
        )

    def send_colour(s):
        return pltpu.make_async_remote_copy(
            src_ref=colour.at[0, :, :, columns(2 * s + 1 - c)],
            dst_ref=cols.at[c, s],
            send_sem=c_send.at[s],
            recv_sem=c_recv.at[s],
            device_id=(sibling, t),
            device_id_type=MESH,
        )

    def recv_colour(s):
        return pltpu.make_async_remote_copy(
            src_ref=colour.at[0, :, :, columns(2 * s + 1 - c)],
            dst_ref=cols.at[1 - c, s],
            send_sem=c_send.at[s],
            recv_sem=c_recv.at[s],
            device_id=(sibling, t),
            device_id_type=MESH,
        )

    def send_remain(k, j):
        to = chip(sigma * j)
        first = 1 if j in (4, 5) else 0
        return pltpu.make_async_remote_copy(
            src_ref=remain_out.at[k, j, pl.ds(first, 2 - first)],
            dst_ref=remain_in.at[k, j, pl.ds(first, 2 - first)],
            send_sem=r_send.at[k, j],
            recv_sem=r_recv.at[k, j],
            device_id=(2 * to + c, t),
            device_id_type=MESH,
        )

    def send_part(k, j):
        to = chip(-sigma) if j <= 4 else chip(sigma)
        return pltpu.make_async_remote_copy(
            src_ref=part_out.at[k, j],
            dst_ref=part_in.at[k, j - 1 if j <= 4 else j + 1],
            send_sem=p_send.at[k, j],
            recv_sem=p_recv.at[k, j - 1 if j <= 4 else j + 1],
            device_id=(2 * to + c, t),
            device_id_type=MESH,
        )

    def recv_part(k, slot):
        return pltpu.make_async_remote_copy(
            src_ref=part_out.at[k, 1],
            dst_ref=part_in.at[k, slot],
            send_sem=p_send.at[k, 1],
            recv_sem=p_recv.at[k, slot],
            device_id=(sibling, t),
            device_id_type=MESH,
        )

    def send_halo(k, side):
        middle = window.at[:, pl.ds(pl.multiple_of(height + k * chunk, chunk), chunk), :]
        at = 2 * height if side == 0 else 0
        return pltpu.make_async_remote_copy(
            src_ref=middle,
            dst_ref=window.at[:, pl.ds(pl.multiple_of(at + k * chunk, chunk), chunk), :],
            send_sem=h_send.at[k, side],
            recv_sem=h_recv.at[k, side],
            device_id=(d, above if side == 0 else below),
            device_id_type=MESH,
        )

    def send_beside(channel, side):
        to = (d + GROUPS - 1) % GROUPS if side == 0 else (d + 1) % GROUPS
        source = HC if side == 0 else slab
        target = HC + slab if side == 0 else 0
        return pltpu.make_async_remote_copy(
            src_ref=vert.at[channel, :, pl.ds(source, HC)],
            dst_ref=vert.at[channel, :, pl.ds(target, HC)],
            send_sem=v_send.at[channel, side],
            recv_sem=v_recv.at[channel, side],
            device_id=(to, t),
            device_id_type=MESH,
        )

    def every(first, last, body):
        def outer(k, _):
            def inner(i, _):
                body(k, i)
                return 0

            return lax.fori_loop(first, last, inner, 0)

        lax.fori_loop(0, CHUNKS, outer, 0)

    every(1, GROUPS, lambda k, i: send_alpha(k, i).start())
    loop(CHIPS, lambda s: send_colour(s).start())

    for copy in small:
        copy.wait()
    flips = [(order[0] // (1 << bit)) % 2 for bit in range(4)]

    place = lax.broadcasted_iota(jnp.int32, (3 * height, height), 0)
    picks = jnp.zeros((3 * height, height), F32)
    for tap in range(4):
        taps = row_taps[tap, :][None, :]
        picks += jnp.where(taps == place, row_weights[tap, :].astype(F32)[None, :], 0.0)
    outside = ((place < height) & (t == 0)) | ((place >= 2 * height) & (t == tiles - 1))
    row_picks[...] = jnp.transpose(jnp.where(outside, 0.0, picks)).astype(BF16)

    width = slab + 2 * HC
    p = t // bands_per_projector
    place = lax.broadcasted_iota(jnp.int32, (width, slab), 0) + (d * slab - HC)
    col_picks = jnp.zeros((width, slab), F32)
    for tap in range(4):
        taps = col_taps[p, tap, :][None, :]
        col_picks += jnp.where(taps == place, col_weights[p, tap, :].astype(F32)[None, :], 0.0)
    col_matrix[...] = col_picks.astype(BF16)


    def in_front(bit, value, hidden):
        return jnp.where(flips[bit] == value, 1.0, hidden)

    def block_at(b):
        lanes = slab // LANES
        return (
            pl.multiple_of((b // lanes) * TILE_ROWS, TILE_ROWS),
            pl.multiple_of((b % lanes) * LANES, LANES),
        )

    def remains(k):
        own_alpha(k).wait()
        loop(GROUPS - 1, lambda i: recv_alpha(k, i + 1).wait_recv())

        def block(b):
            row, lane = block_at(b)
            place = (pl.ds(row, TILE_ROWS), pl.ds(lane, LANES))
            clear = [1.0 - opac[(k, g) + place].astype(F32) for g in range(GROUPS)]
            eight = [clear[g] * clear[g + 8] for g in range(8)]
            four = [eight[g] * eight[g + 4] for g in range(4)]
            two = [four[g] * four[g + 2] for g in range(2)]
            left = [in_front(0, g, two[1 - g]) for g in range(2)]
            left = [left[g % 2] * in_front(1, g // 2, four[g ^ 2]) for g in range(4)]
            left = [left[g % 4] * in_front(2, g // 4, eight[g ^ 4]) for g in range(8)]
            for g in range(GROUPS):
                left_all[g] = left[g % 8] * in_front(3, g // 8, clear[g ^ 8])
            kept[(k, 0) + place] = left_all[2 * y]
            kept[(k, 1) + place] = left_all[2 * y + 1]
            for j, ends in (((4, 3, 2, 1), 2), ((5, 6, 7), 3)):
                scale = left_all[2 * chip(sigma * j[0])]
                kept[(k, ends) + place] = scale
                scale = 1.0 / scale
                for i in j:
                    for core in range(2):
                        if i != j[0] or core:
                            value = left_all[2 * chip(sigma * i) + core] * scale
                            remain_out[(k, i, core) + place] = (value * value).astype(BF16)

        loop(blocks, block)
        for j in STEPS:
            send_remain(k, j).start()

    loop(CHUNKS, remains)

    loop(CHIPS, lambda s: own_colour(s).wait())
    loop(CHIPS, lambda s: recv_colour(s).wait_recv())
    loop(CHIPS, lambda s: send_colour(s).wait_send())
    every(1, GROUPS, lambda k, i: send_alpha(k, i).wait_send())

    def add_step(j):
        s = chip(-sigma * j)

        def of_chunk(k):
            send_remain(k, j).wait_recv()
            if j not in (4, 5):
                recv_part(k, j).wait_recv()

            def block(b):
                row, lane = block_at(b)
                place = (pl.ds(row, TILE_ROWS), pl.ds(lane, LANES))
                whole = (pl.ds(pl.multiple_of(k * chunk + row, TILE_ROWS), TILE_ROWS), pl.ds(lane, LANES))
                if j not in (4, 5):
                    first = root(remain_in[(k, j, 0) + place])
                second = root(remain_in[(k, j, 1) + place])
                for channel in range(3):
                    total = cols[(0, s, channel) + whole].astype(F32)
                    if j not in (4, 5):
                        total = first * total
                    total += second * cols[(1, s, channel) + whole].astype(F32)
                    if j not in (4, 5):
                        total += root(part_in[(k, j, channel) + place])
                    part_out[(k, j, channel) + place] = square(total)

            loop(blocks, block)
            send_part(k, j).start()

        loop(CHUNKS, of_chunk)

    for j in STEPS:
        add_step(j)

    def finish(k):
        recv_part(k, 0).wait_recv()
        recv_part(k, 8).wait_recv()

        def block(b):
            row, lane = block_at(b)
            place = (pl.ds(row, TILE_ROWS), pl.ds(lane, LANES))
            whole_row = pl.multiple_of(k * chunk + row, TILE_ROWS)
            whole = (pl.ds(whole_row, TILE_ROWS), pl.ds(lane, LANES))
            middle = (pl.ds(pl.multiple_of(height + whole_row, TILE_ROWS), TILE_ROWS), pl.ds(lane, LANES))
            first, second = kept[(k, 0) + place], kept[(k, 1) + place]
            far, near = kept[(k, 2) + place], kept[(k, 3) + place]
            for channel in range(3):
                total = first * cols[(0, y, channel) + whole].astype(F32)
                total += second * cols[(1, y, channel) + whole].astype(F32)
                total += far * root(part_in[(k, 0, channel) + place])
                total += near * root(part_in[(k, 8, channel) + place])
                high = total.astype(BF16)
                window[(channel,) + middle] = high
                low[(channel,) + whole] = (total - high.astype(F32)).astype(BF16)

        loop(blocks, block)
        send_halo(k, 0).start()
        send_halo(k, 1).start()

    loop(CHUNKS, finish)

    for j in STEPS:
        loop(CHUNKS, lambda k: send_remain(k, j).wait_send())
        loop(CHUNKS, lambda k: send_part(k, j).wait_send())

    def wait_halo(k):
        send_halo(k, 0).wait_recv()
        send_halo(k, 1).wait_recv()

    def product(a, b):
        return jnp.dot(a, b, preferred_element_type=F32)

    for channel in range(3):
        band = row_picks[:, height : 2 * height]
        partial[channel] = product(band, window[channel, height : 2 * height]) + product(
            band, low[channel]
        )
    loop(CHUNKS, wait_halo)

    for channel in range(3):
        value = partial[channel]
        value += product(row_picks[:, :height], window[channel, :height])
        value += product(row_picks[:, 2 * height :], window[channel, 2 * height :])
        vert[channel, :, HC : HC + slab] = value.astype(BF16)
        for side in range(2):
            send_beside(channel, side).start()
    for channel in range(3):
        partial[channel] = product(
            vert[channel, :, HC : HC + slab], col_matrix[HC : HC + slab]
        )

    within = (t % bands_per_projector) * height + lax.broadcasted_iota(jnp.int32, (height, slab), 0)
    within = within.astype(F32)
    proj_height = bands_per_projector * height
    ramp = jnp.minimum(
        1.0, jnp.minimum((within + 0.5) / BLEND, (proj_height - within - 0.5) / BLEND)
    )

    blended = []
    for channel in range(3):
        for side in range(2):
            send_beside(channel, side).wait_recv()
        value = partial[channel]
        value += product(vert[channel, :, :HC], col_matrix[:HC])
        value += product(vert[channel, :, HC + slab :], col_matrix[HC + slab :])
        blended.append(value * ramp)
    for channel in range(3):
        mixed = matrix[channel, p, 0] * blended[0]
        mixed += matrix[channel, p, 1] * blended[1]
        mixed += matrix[channel, p, 2] * blended[2]
        out[channel] = mixed + offsets[p, channel]

    loop(CHUNKS, lambda k: send_halo(k, 0).wait_send())
    loop(CHUNKS, lambda k: send_halo(k, 1).wait_send())
    for channel in range(3):
        for side in range(2):
            send_beside(channel, side).wait_send()


def shards(
    colour, alpha, depth_order, row_taps, row_weights, col_taps, col_weights, colour_matrix, offsets
):
    tiles = lax.axis_size("tile")
    height = colour.shape[2]
    slab = colour.shape[3] // GROUPS
    chunk = height // CHUNKS
    hbm = pl.BlockSpec(memory_space=pltpu.HBM)
    vmem = pl.BlockSpec(memory_space=pltpu.VMEM)
    matrix = jnp.transpose(colour_matrix, (1, 0, 2))
    dma = pltpu.SemaphoreType.DMA
    return pl.pallas_call(
        functools.partial(kernel, tiles // colour_matrix.shape[0], tiles),
        out_shape=jax.ShapeDtypeStruct((3, height, slab), F32),
        in_specs=[hbm] * 9,
        out_specs=vmem,
        scratch_shapes=[
            pltpu.SMEM(depth_order.shape, depth_order.dtype),
            pltpu.VMEM(row_taps.shape, row_taps.dtype),
            pltpu.VMEM(row_weights.shape, row_weights.dtype),
            pltpu.VMEM(col_taps.shape, col_taps.dtype),
            pltpu.VMEM(col_weights.shape, col_weights.dtype),
            pltpu.SMEM(matrix.shape, matrix.dtype),
            pltpu.SMEM(offsets.shape, offsets.dtype),
            pltpu.VMEM((CHUNKS, GROUPS, chunk, slab), BF16),
            pltpu.VMEM((2, CHIPS, 3, height, slab), BF16),
            pltpu.VMEM((GROUPS, TILE_ROWS, LANES), F32),
            pltpu.VMEM((CHUNKS, 4, chunk, slab), F32),
            pltpu.VMEM((CHUNKS, CHIPS, 2, chunk, slab), BF16),
            pltpu.VMEM((CHUNKS, CHIPS, 2, chunk, slab), BF16),
            pltpu.VMEM((CHUNKS, CHIPS, 3, chunk, slab), BF16),
            pltpu.VMEM((CHUNKS, CHIPS + 1, 3, chunk, slab), BF16),
            pltpu.VMEM((3, 3 * height, slab), BF16),
            pltpu.VMEM((3, height, slab), BF16),
            pltpu.VMEM((3, height, slab + 2 * HC), BF16),
            pltpu.VMEM((height, 3 * height), BF16),
            pltpu.VMEM((slab + 2 * HC, slab), BF16),
            pltpu.VMEM((3, height, slab), F32),
            dma((CHUNKS, GROUPS)),
            dma((CHUNKS, GROUPS)),
            dma((CHUNKS,)),
            dma((CHIPS,)),
            dma((CHIPS,)),
            dma((CHIPS,)),
            dma((CHUNKS, CHIPS)),
            dma((CHUNKS, CHIPS)),
            dma((CHUNKS, CHIPS)),
            dma((CHUNKS, CHIPS + 1)),
            dma((CHUNKS, 2)),
            dma((CHUNKS, 2)),
            dma((3, 2)),
            dma((3, 2)),
            dma((7,)),
        ],
        compiler_params=pltpu.CompilerParams(
            collective_id=0, has_side_effects=True, vmem_limit_bytes=40 * 2**20
        ),
    )(*[
        pltpu.with_memory_space_constraint(x, pltpu.HBM)
        for x in (
            colour, alpha, depth_order, row_taps, row_weights, col_taps, col_weights, matrix, offsets
        )
    ])


def solution(mesh):
    return jax.shard_map(
        shards,
        mesh=mesh,
        in_specs=(
            P("depth", None, "tile", None),
            P("depth", "tile", None),
            P(),
            P(None, "tile"),
            P(None, "tile"),
            P(None, None, "depth"),
            P(None, None, "depth"),
            P(),
            P(),
        ),
        out_specs=P(None, "tile", "depth"),
        check_vma=False,
    )
```

```python
import functools

import jax
import jax.numpy as jnp
from jax import lax
from jax.experimental import pallas as pl
from jax.experimental.pallas import tpu as pltpu
from jax.sharding import PartitionSpec as P

HC = 128
BLEND = 64
GROUPS = 16
CHIPS = 8
CHUNKS = 4
COARSE = 2
TILE_ROWS = 16
LANES = 128
STEPS = (4, 5, 3, 6, 2, 7, 1)
MESH = pl.DeviceIdType.MESH
F32 = jnp.float32
BF16 = jnp.bfloat16


def square(x):
    return (x * jnp.abs(x)).astype(BF16)


def root(v):
    v = v.astype(F32)
    return v * lax.rsqrt(jnp.maximum(jnp.abs(v), 1e-37))


def kernel(
    bands_per_projector,
    tiles,
    colour, alpha, order_in, row_taps_in, row_weights_in, col_taps_in, col_weights_in, matrix_in,
    offsets_in,
    out,
    order, row_taps, row_weights, col_taps, col_weights, matrix, offsets,
    opac, cols, left_all, kept, remain_out, remain_in, part_out, part_in, window, low, vert,
    row_picks, col_matrix, partial,
    a_send, a_recv, a_own, c_own, c_send, c_recv, r_send, r_recv, p_send, p_recv,
    h_send, h_recv, v_send, v_recv, s_own,
):
    height, slab = out.shape[1], out.shape[2]
    chunk = height // CHUNKS
    coarse = height // COARSE
    blocks = (chunk // TILE_ROWS) * (slab // LANES)
    d = lax.axis_index("depth")
    t = lax.axis_index("tile")
    y, c = d // 2, d % 2
    sigma = 1 - 2 * c
    sibling = 2 * y + 1 - c
    below, above = (t + 1) % tiles, (t + tiles - 1) % tiles

    def chip(offset):
        return (y + offset + 2 * CHIPS) % CHIPS

    def columns(device):
        return pl.ds(pl.multiple_of(device * slab, slab), slab)

    def rows_of(k):
        return pl.ds(pl.multiple_of(k * coarse, coarse), coarse)

    barrier = pltpu.get_barrier_semaphore()

    def greet(i, _):
        pl.semaphore_signal(barrier, 1, device_id=((d + i) % GROUPS, t), device_id_type=MESH)
        return 0

    lax.fori_loop(1, GROUPS, greet, 0)
    pl.semaphore_signal(barrier, 1, device_id=(d, below), device_id_type=MESH)
    pl.semaphore_signal(barrier, 1, device_id=(d, above), device_id_type=MESH)

    def own_alpha(k):
        return pltpu.make_async_copy(
            alpha.at[0, rows_of(k), columns(d)], opac.at[k, d], a_own.at[k]
        )

    def own_colour(s):
        return pltpu.make_async_copy(
            colour.at[0, :, :, columns(2 * s + c)], cols.at[c, s], c_own.at[s]
        )

    def loop(n, body):
        def step(i, _):
            body(i)
            return 0

        lax.fori_loop(0, n, step, 0)

    small = [
        pltpu.make_async_copy(source, target, s_own.at[i])
        for i, (source, target) in enumerate((
            (order_in, order),
            (row_taps_in, row_taps),
            (row_weights_in, row_weights),
            (col_taps_in, col_taps),
            (col_weights_in, col_weights),
            (matrix_in, matrix),
            (offsets_in, offsets),
        ))
    ]
    for copy in small:
        copy.start()
    loop(COARSE, lambda k: own_alpha(k).start())
    loop(CHIPS, lambda s: own_colour(s).start())
    pl.semaphore_wait(barrier, GROUPS + 1)

    def send_alpha(k, i):
        to = (d + i) % GROUPS
        return pltpu.make_async_remote_copy(
            src_ref=alpha.at[0, rows_of(k), columns(to)],
            dst_ref=opac.at[k, d],
            send_sem=a_send.at[k, i],
            recv_sem=a_recv.at[k, i],
            device_id=(to, t),
            device_id_type=MESH,
        )

    def recv_alpha(k, i):
        source = (d + GROUPS - i) % GROUPS
        return pltpu.make_async_remote_copy(
            src_ref=alpha.at[0, rows_of(k), columns(source)],
            dst_ref=opac.at[k, source],
            send_sem=a_send.at[k, i],
            recv_sem=a_recv.at[k, i],
            device_id=(source, t),
            device_id_type=MESH,
        )

    def send_colour(s):
        return pltpu.make_async_remote_copy(
            src_ref=colour.at[0, :, :, columns(2 * s + 1 - c)],
            dst_ref=cols.at[c, s],
            send_sem=c_send.at[s],
            recv_sem=c_recv.at[s],
            device_id=(sibling, t),
            device_id_type=MESH,
        )

    def recv_colour(s):
        return pltpu.make_async_remote_copy(
            src_ref=colour.at[0, :, :, columns(2 * s + 1 - c)],
            dst_ref=cols.at[1 - c, s],
            send_sem=c_send.at[s],
            recv_sem=c_recv.at[s],
            device_id=(sibling, t),
            device_id_type=MESH,
        )

    def send_remain(k, j):
        to = chip(sigma * j)
        first = 1 if j in (4, 5) else 0
        return pltpu.make_async_remote_copy(
            src_ref=remain_out.at[k, j, pl.ds(first, 2 - first)],
            dst_ref=remain_in.at[k, j, pl.ds(first, 2 - first)],
            send_sem=r_send.at[k, j],
            recv_sem=r_recv.at[k, j],
            device_id=(2 * to + c, t),
            device_id_type=MESH,
        )

    def send_part(k, j):
        to = chip(-sigma) if j <= 4 else chip(sigma)
        return pltpu.make_async_remote_copy(
            src_ref=part_out.at[k, j],
            dst_ref=part_in.at[k, j - 1 if j <= 4 else j + 1],
            send_sem=p_send.at[k, j],
            recv_sem=p_recv.at[k, j - 1 if j <= 4 else j + 1],
            device_id=(2 * to + c, t),
            device_id_type=MESH,
        )

    def recv_part(k, slot):
        return pltpu.make_async_remote_copy(
            src_ref=part_out.at[k, 1],
            dst_ref=part_in.at[k, slot],
            send_sem=p_send.at[k, 1],
            recv_sem=p_recv.at[k, slot],
            device_id=(sibling, t),
            device_id_type=MESH,
        )

    def send_halo(k, side):
        middle = window.at[:, pl.ds(pl.multiple_of(height + k * chunk, chunk), chunk), :]
        at = 2 * height if side == 0 else 0
        return pltpu.make_async_remote_copy(
            src_ref=middle,
            dst_ref=window.at[:, pl.ds(pl.multiple_of(at + k * chunk, chunk), chunk), :],
            send_sem=h_send.at[k, side],
            recv_sem=h_recv.at[k, side],
            device_id=(d, above if side == 0 else below),
            device_id_type=MESH,
        )

    def send_beside(channel, side):
        to = (d + GROUPS - 1) % GROUPS if side == 0 else (d + 1) % GROUPS
        source = HC if side == 0 else slab
        target = HC + slab if side == 0 else 0
        return pltpu.make_async_remote_copy(
            src_ref=vert.at[channel, :, pl.ds(source, HC)],
            dst_ref=vert.at[channel, :, pl.ds(target, HC)],
            send_sem=v_send.at[channel, side],
            recv_sem=v_recv.at[channel, side],
            device_id=(to, t),
            device_id_type=MESH,
        )

    def every(first, last, body):
        def outer(k, _):
            def inner(i, _):
                body(k, i)
                return 0

            return lax.fori_loop(first, last, inner, 0)

        lax.fori_loop(0, COARSE, outer, 0)

    every(1, GROUPS, lambda k, i: send_alpha(k, i).start())
    loop(CHIPS, lambda s: send_colour(s).start())

    for copy in small:
        copy.wait()
    flips = [(order[0] // (1 << bit)) % 2 for bit in range(4)]

    place = lax.broadcasted_iota(jnp.int32, (3 * height, height), 0)
    picks = jnp.zeros((3 * height, height), F32)
    for tap in range(4):
        taps = row_taps[tap, :][None, :]
        picks += jnp.where(taps == place, row_weights[tap, :].astype(F32)[None, :], 0.0)
    outside = ((place < height) & (t == 0)) | ((place >= 2 * height) & (t == tiles - 1))
    row_picks[...] = jnp.transpose(jnp.where(outside, 0.0, picks)).astype(BF16)

    width = slab + 2 * HC
    p = t // bands_per_projector
    place = lax.broadcasted_iota(jnp.int32, (width, slab), 0) + (d * slab - HC)
    col_picks = jnp.zeros((width, slab), F32)
    for tap in range(4):
        taps = col_taps[p, tap, :][None, :]
        col_picks += jnp.where(taps == place, col_weights[p, tap, :].astype(F32)[None, :], 0.0)
    col_matrix[...] = col_picks.astype(BF16)


    def in_front(bit, value, hidden):
        return jnp.where(flips[bit] == value, 1.0, hidden)

    def block_at(b):
        lanes = slab // LANES
        return (
            pl.multiple_of((b // lanes) * TILE_ROWS, TILE_ROWS),
            pl.multiple_of((b % lanes) * LANES, LANES),
        )

    def remains(k):
        own_alpha(k).wait()
        loop(GROUPS - 1, lambda i: recv_alpha(k, i + 1).wait_recv())

        def block(b):
            row, lane = block_at(b)
            place = (pl.ds(row, TILE_ROWS), pl.ds(lane, LANES))
            clear = [1.0 - opac[(k, g) + place].astype(F32) for g in range(GROUPS)]
            eight = [clear[g] * clear[g + 8] for g in range(8)]
            four = [eight[g] * eight[g + 4] for g in range(4)]
            two = [four[g] * four[g + 2] for g in range(2)]
            left = [in_front(0, g, two[1 - g]) for g in range(2)]
            left = [left[g % 2] * in_front(1, g // 2, four[g ^ 2]) for g in range(4)]
            left = [left[g % 4] * in_front(2, g // 4, eight[g ^ 4]) for g in range(8)]
            for g in range(GROUPS):
                left_all[g] = left[g % 8] * in_front(3, g // 8, clear[g ^ 8])
            kept[(k, 0) + place] = left_all[2 * y]
            kept[(k, 1) + place] = left_all[2 * y + 1]
            for j, ends in (((4, 3, 2, 1), 2), ((5, 6, 7), 3)):
                scale = left_all[2 * chip(sigma * j[0])]
                kept[(k, ends) + place] = scale
                scale = 1.0 / scale
                for i in j:
                    for core in range(2):
                        if i != j[0] or core:
                            value = left_all[2 * chip(sigma * i) + core] * scale
                            remain_out[(k, i, core) + place] = (value * value).astype(BF16)

        loop(blocks * (CHUNKS // COARSE), block)
        for j in STEPS:
            send_remain(k, j).start()

    loop(COARSE, remains)

    loop(CHIPS, lambda s: own_colour(s).wait())
    loop(CHIPS, lambda s: recv_colour(s).wait_recv())
    loop(CHIPS, lambda s: send_colour(s).wait_send())
    every(1, GROUPS, lambda k, i: send_alpha(k, i).wait_send())

    def within_coarse(k, row, lane):
        start = (k % (CHUNKS // COARSE)) * chunk + row
        return (pl.ds(pl.multiple_of(start, TILE_ROWS), TILE_ROWS), pl.ds(lane, LANES))

    def add_step(j):
        s = chip(-sigma * j)

        def of_chunk(q, k):
            if j not in (4, 5):
                recv_part(k, j).wait_recv()

            def block(b):
                row, lane = block_at(b)
                place = (pl.ds(row, TILE_ROWS), pl.ds(lane, LANES))
                whole = (pl.ds(pl.multiple_of(k * chunk + row, TILE_ROWS), TILE_ROWS), pl.ds(lane, LANES))
                inner = within_coarse(k, row, lane)
                if j not in (4, 5):
                    first = root(remain_in[(q, j, 0) + inner])
                second = root(remain_in[(q, j, 1) + inner])
                for channel in range(3):
                    total = cols[(0, s, channel) + whole].astype(F32)
                    if j not in (4, 5):
                        total = first * total
                    total += second * cols[(1, s, channel) + whole].astype(F32)
                    if j not in (4, 5):
                        total += root(part_in[(k, j, channel) + place])
                    part_out[(k, j, channel) + place] = square(total)

            loop(blocks, block)
            send_part(k, j).start()

        def at(k):
            if k % (CHUNKS // COARSE) == 0:
                send_remain(k // (CHUNKS // COARSE), j).wait_recv()
            of_chunk(k // (CHUNKS // COARSE), k)

        return at

    bodies = [add_step(j) for j in STEPS]
    for _, k, i in sorted((i + 0.5 * k, k, i) for i in range(7) for k in range(CHUNKS)):
        bodies[i](k)

    def finish(k):
        recv_part(k, 0).wait_recv()
        recv_part(k, 8).wait_recv()

        def block(b):
            row, lane = block_at(b)
            place = (pl.ds(row, TILE_ROWS), pl.ds(lane, LANES))
            whole_row = pl.multiple_of(k * chunk + row, TILE_ROWS)
            whole = (pl.ds(whole_row, TILE_ROWS), pl.ds(lane, LANES))
            middle = (pl.ds(pl.multiple_of(height + whole_row, TILE_ROWS), TILE_ROWS), pl.ds(lane, LANES))
            q = k // (CHUNKS // COARSE)
            inner = within_coarse(k, row, lane)
            first, second = kept[(q, 0) + inner], kept[(q, 1) + inner]
            far, near = kept[(q, 2) + inner], kept[(q, 3) + inner]
            for channel in range(3):
                total = first * cols[(0, y, channel) + whole].astype(F32)
                total += second * cols[(1, y, channel) + whole].astype(F32)
                total += far * root(part_in[(k, 0, channel) + place])
                total += near * root(part_in[(k, 8, channel) + place])
                high = total.astype(BF16)
                window[(channel,) + middle] = high
                low[(channel,) + whole] = (total - high.astype(F32)).astype(BF16)

        loop(blocks, block)
        send_halo(k, 0).start()
        send_halo(k, 1).start()

    loop(CHUNKS, finish)

    for j in STEPS:
        loop(COARSE, lambda k: send_remain(k, j).wait_send())
        loop(CHUNKS, lambda k: send_part(k, j).wait_send())

    def wait_halo(k):
        send_halo(k, 0).wait_recv()
        send_halo(k, 1).wait_recv()

    def product(a, b):
        return jnp.dot(a, b, preferred_element_type=F32)

    for channel in range(3):
        band = row_picks[:, height : 2 * height]
        partial[channel] = product(band, window[channel, height : 2 * height]) + product(
            band, low[channel]
        )
    loop(CHUNKS, wait_halo)

    for channel in range(3):
        value = partial[channel]
        value += product(row_picks[:, :height], window[channel, :height])
        value += product(row_picks[:, 2 * height :], window[channel, 2 * height :])
        vert[channel, :, HC : HC + slab] = value.astype(BF16)
        for side in range(2):
            send_beside(channel, side).start()
    for channel in range(3):
        partial[channel] = product(
            vert[channel, :, HC : HC + slab], col_matrix[HC : HC + slab]
        )

    within = (t % bands_per_projector) * height + lax.broadcasted_iota(jnp.int32, (height, slab), 0)
    within = within.astype(F32)
    proj_height = bands_per_projector * height
    ramp = jnp.minimum(
        1.0, jnp.minimum((within + 0.5) / BLEND, (proj_height - within - 0.5) / BLEND)
    )

    blended = []
    for channel in range(3):
        for side in range(2):
            send_beside(channel, side).wait_recv()
        value = jnp.concatenate(
            [
                product(vert[channel, :, :HC], col_matrix[:HC, :HC]),
                product(vert[channel, :, HC + slab :], col_matrix[HC + slab :, HC:]),
            ],
            axis=1,
        )
        blended.append((partial[channel] + value) * ramp)
    for channel in range(3):
        mixed = matrix[channel, p, 0] * blended[0]
        mixed += matrix[channel, p, 1] * blended[1]
        mixed += matrix[channel, p, 2] * blended[2]
        out[channel] = mixed + offsets[p, channel]

    loop(CHUNKS, lambda k: send_halo(k, 0).wait_send())
    loop(CHUNKS, lambda k: send_halo(k, 1).wait_send())
    for channel in range(3):
        for side in range(2):
            send_beside(channel, side).wait_send()


def shards(
    colour, alpha, depth_order, row_taps, row_weights, col_taps, col_weights, colour_matrix, offsets
):
    tiles = lax.axis_size("tile")
    height = colour.shape[2]
    slab = colour.shape[3] // GROUPS
    chunk, coarse = height // CHUNKS, height // COARSE
    hbm = pl.BlockSpec(memory_space=pltpu.HBM)
    vmem = pl.BlockSpec(memory_space=pltpu.VMEM)
    matrix = jnp.transpose(colour_matrix, (1, 0, 2))
    dma = pltpu.SemaphoreType.DMA
    return pl.pallas_call(
        functools.partial(kernel, tiles // colour_matrix.shape[0], tiles),
        out_shape=jax.ShapeDtypeStruct((3, height, slab), F32),
        in_specs=[hbm] * 9,
        out_specs=vmem,
        scratch_shapes=[
            pltpu.SMEM(depth_order.shape, depth_order.dtype),
            pltpu.VMEM(row_taps.shape, row_taps.dtype),
            pltpu.VMEM(row_weights.shape, row_weights.dtype),
            pltpu.VMEM(col_taps.shape, col_taps.dtype),
            pltpu.VMEM(col_weights.shape, col_weights.dtype),
            pltpu.SMEM(matrix.shape, matrix.dtype),
            pltpu.SMEM(offsets.shape, offsets.dtype),
            pltpu.VMEM((COARSE, GROUPS, coarse, slab), BF16),
            pltpu.VMEM((2, CHIPS, 3, height, slab), BF16),
            pltpu.VMEM((GROUPS, TILE_ROWS, LANES), F32),
            pltpu.VMEM((COARSE, 4, coarse, slab), F32),
            pltpu.VMEM((COARSE, CHIPS, 2, coarse, slab), BF16),
            pltpu.VMEM((COARSE, CHIPS, 2, coarse, slab), BF16),
            pltpu.VMEM((CHUNKS, CHIPS, 3, chunk, slab), BF16),
            pltpu.VMEM((CHUNKS, CHIPS + 1, 3, chunk, slab), BF16),
            pltpu.VMEM((3, 3 * height, slab), BF16),
            pltpu.VMEM((3, height, slab), BF16),
            pltpu.VMEM((3, height, slab + 2 * HC), BF16),
            pltpu.VMEM((height, 3 * height), BF16),
            pltpu.VMEM((slab + 2 * HC, slab), BF16),
            pltpu.VMEM((3, height, slab), F32),
            dma((COARSE, GROUPS)),
            dma((COARSE, GROUPS)),
            dma((COARSE,)),
            dma((CHIPS,)),
            dma((CHIPS,)),
            dma((CHIPS,)),
            dma((COARSE, CHIPS)),
            dma((COARSE, CHIPS)),
            dma((CHUNKS, CHIPS)),
            dma((CHUNKS, CHIPS + 1)),
            dma((CHUNKS, 2)),
            dma((CHUNKS, 2)),
            dma((3, 2)),
            dma((3, 2)),
            dma((7,)),
        ],
        compiler_params=pltpu.CompilerParams(
            collective_id=0, has_side_effects=True, vmem_limit_bytes=40 * 2**20
        ),
    )(*[
        pltpu.with_memory_space_constraint(x, pltpu.HBM)
        for x in (
            colour, alpha, depth_order, row_taps, row_weights, col_taps, col_weights, matrix, offsets
        )
    ])


def solution(mesh):
    return jax.shard_map(
        shards,
        mesh=mesh,
        in_specs=(
            P("depth", None, "tile", None),
            P("depth", "tile", None),
            P(),
            P(None, "tile"),
            P(None, "tile"),
            P(None, None, "depth"),
            P(None, None, "depth"),
            P(),
            P(),
        ),
        out_specs=P(None, "tile", "depth"),
        check_vma=False,
    )
```

```python
import functools

import jax
import jax.numpy as jnp
from jax import lax
from jax.experimental import pallas as pl
from jax.experimental.pallas import tpu as pltpu
from jax.sharding import PartitionSpec as P

HC = 128
BLEND = 64
GROUPS = 16
CHIPS = 8
CHUNKS = 4
COARSE = 2
TILE_ROWS = 16
LANES = 128
STEPS = (4, 5, 3, 6, 2, 7, 1)
MESH = pl.DeviceIdType.MESH
F32 = jnp.float32
BF16 = jnp.bfloat16


def square(x):
    return (x * jnp.abs(x)).astype(BF16)


def root(v):
    v = v.astype(F32)
    return v * lax.rsqrt(jnp.maximum(jnp.abs(v), 1e-37))


def kernel(
    bands_per_projector,
    tiles,
    colour, alpha, order_in, row_taps_in, row_weights_in, col_taps_in, col_weights_in, matrix_in,
    offsets_in,
    out,
    order, row_taps, row_weights, col_taps, col_weights, matrix, offsets,
    opac, cols, left_all, kept, remain_out, remain_in, part_out, part_in, window, low, vert,
    row_picks, col_matrix, partial,
    a_send, a_recv, a_own, c_own, c_send, c_recv, r_send, r_recv, p_send, p_recv,
    h_send, h_recv, v_send, v_recv, s_own,
):
    height, slab = out.shape[1], out.shape[2]
    chunk = height // CHUNKS
    coarse = height // COARSE
    blocks = (chunk // TILE_ROWS) * (slab // LANES)
    d = lax.axis_index("depth")
    t = lax.axis_index("tile")
    y, c = d // 2, d % 2
    sigma = 1 - 2 * c
    sibling = 2 * y + 1 - c
    below, above = (t + 1) % tiles, (t + tiles - 1) % tiles

    def chip(offset):
        return (y + offset + 2 * CHIPS) % CHIPS

    def columns(device):
        return pl.ds(pl.multiple_of(device * slab, slab), slab)

    def rows_of(k):
        return pl.ds(pl.multiple_of(k * coarse, coarse), coarse)

    barrier = pltpu.get_barrier_semaphore()

    def greet(i, _):
        pl.semaphore_signal(barrier, 1, device_id=((d + i) % GROUPS, t), device_id_type=MESH)
        return 0

    lax.fori_loop(1, GROUPS, greet, 0)
    pl.semaphore_signal(barrier, 1, device_id=(d, below), device_id_type=MESH)
    pl.semaphore_signal(barrier, 1, device_id=(d, above), device_id_type=MESH)

    def own_alpha(k):
        return pltpu.make_async_copy(
            alpha.at[0, rows_of(k), columns(d)], opac.at[k, d], a_own.at[k]
        )

    def own_colour(s):
        return pltpu.make_async_copy(
            colour.at[0, :, :, columns(2 * s + c)], cols.at[c, s], c_own.at[s]
        )

    def loop(n, body):
        def step(i, _):
            body(i)
            return 0

        lax.fori_loop(0, n, step, 0)

    small = [
        pltpu.make_async_copy(source, target, s_own.at[i])
        for i, (source, target) in enumerate((
            (order_in, order),
            (row_taps_in, row_taps),
            (row_weights_in, row_weights),
            (col_taps_in, col_taps),
            (col_weights_in, col_weights),
            (matrix_in, matrix),
            (offsets_in, offsets),
        ))
    ]
    pl.semaphore_wait(barrier, GROUPS + 1)

    def send_alpha(k, i):
        to = (d + i) % GROUPS
        return pltpu.make_async_remote_copy(
            src_ref=alpha.at[0, rows_of(k), columns(to)],
            dst_ref=opac.at[k, d],
            send_sem=a_send.at[k, i],
            recv_sem=a_recv.at[k, i],
            device_id=(to, t),
            device_id_type=MESH,
        )

    def recv_alpha(k, i):
        source = (d + GROUPS - i) % GROUPS
        return pltpu.make_async_remote_copy(
            src_ref=alpha.at[0, rows_of(k), columns(source)],
            dst_ref=opac.at[k, source],
            send_sem=a_send.at[k, i],
            recv_sem=a_recv.at[k, i],
            device_id=(source, t),
            device_id_type=MESH,
        )

    def send_colour(s):
        return pltpu.make_async_remote_copy(
            src_ref=colour.at[0, :, :, columns(2 * s + 1 - c)],
            dst_ref=cols.at[c, s],
            send_sem=c_send.at[s],
            recv_sem=c_recv.at[s],
            device_id=(sibling, t),
            device_id_type=MESH,
        )

    def recv_colour(s):
        return pltpu.make_async_remote_copy(
            src_ref=colour.at[0, :, :, columns(2 * s + 1 - c)],
            dst_ref=cols.at[1 - c, s],
            send_sem=c_send.at[s],
            recv_sem=c_recv.at[s],
            device_id=(sibling, t),
            device_id_type=MESH,
        )

    def send_remain(k, j):
        to = chip(sigma * j)
        first = 1 if j in (4, 5) else 0
        return pltpu.make_async_remote_copy(
            src_ref=remain_out.at[k, j, pl.ds(first, 2 - first)],
            dst_ref=remain_in.at[k, j, pl.ds(first, 2 - first)],
            send_sem=r_send.at[k, j],
            recv_sem=r_recv.at[k, j],
            device_id=(2 * to + c, t),
            device_id_type=MESH,
        )

    def send_part(k, j):
        to = chip(-sigma) if j <= 4 else chip(sigma)
        return pltpu.make_async_remote_copy(
            src_ref=part_out.at[k, j],
            dst_ref=part_in.at[k, j - 1 if j <= 4 else j + 1],
            send_sem=p_send.at[k, j],
            recv_sem=p_recv.at[k, j - 1 if j <= 4 else j + 1],
            device_id=(2 * to + c, t),
            device_id_type=MESH,
        )

    def recv_part(k, slot):
        return pltpu.make_async_remote_copy(
            src_ref=part_out.at[k, 1],
            dst_ref=part_in.at[k, slot],
            send_sem=p_send.at[k, 1],
            recv_sem=p_recv.at[k, slot],
            device_id=(sibling, t),
            device_id_type=MESH,
        )

    def send_halo(k, side):
        middle = window.at[:, pl.ds(pl.multiple_of(height + k * chunk, chunk), chunk), :]
        at = 2 * height if side == 0 else 0
        return pltpu.make_async_remote_copy(
            src_ref=middle,
            dst_ref=window.at[:, pl.ds(pl.multiple_of(at + k * chunk, chunk), chunk), :],
            send_sem=h_send.at[k, side],
            recv_sem=h_recv.at[k, side],
            device_id=(d, above if side == 0 else below),
            device_id_type=MESH,
        )

    def send_beside(channel, side):
        to = (d + GROUPS - 1) % GROUPS if side == 0 else (d + 1) % GROUPS
        source = HC if side == 0 else slab
        target = HC + slab if side == 0 else 0
        return pltpu.make_async_remote_copy(
            src_ref=vert.at[channel, :, pl.ds(source, HC)],
            dst_ref=vert.at[channel, :, pl.ds(target, HC)],
            send_sem=v_send.at[channel, side],
            recv_sem=v_recv.at[channel, side],
            device_id=(to, t),
            device_id_type=MESH,
        )

    def every(first, last, body):
        def outer(k, _):
            def inner(i, _):
                body(k, i)
                return 0

            return lax.fori_loop(first, last, inner, 0)

        lax.fori_loop(0, COARSE, outer, 0)

    every(1, GROUPS, lambda k, i: send_alpha(k, i).start())
    for copy in small:
        copy.start()
    loop(COARSE, lambda k: own_alpha(k).start())
    loop(CHIPS, lambda s: own_colour(s).start())
    loop(CHIPS, lambda s: send_colour(s).start())

    for copy in small:
        copy.wait()
    flips = [(order[0] // (1 << bit)) % 2 for bit in range(4)]

    place = lax.broadcasted_iota(jnp.int32, (3 * height, height), 0)
    picks = jnp.zeros((3 * height, height), F32)
    for tap in range(4):
        taps = row_taps[tap, :][None, :]
        picks += jnp.where(taps == place, row_weights[tap, :].astype(F32)[None, :], 0.0)
    outside = ((place < height) & (t == 0)) | ((place >= 2 * height) & (t == tiles - 1))
    row_picks[...] = jnp.transpose(jnp.where(outside, 0.0, picks)).astype(BF16)

    width = slab + 2 * HC
    p = t // bands_per_projector
    place = lax.broadcasted_iota(jnp.int32, (width, slab), 0) + (d * slab - HC)
    col_picks = jnp.zeros((width, slab), F32)
    for tap in range(4):
        taps = col_taps[p, tap, :][None, :]
        col_picks += jnp.where(taps == place, col_weights[p, tap, :].astype(F32)[None, :], 0.0)
    col_matrix[...] = col_picks.astype(BF16)


    def in_front(bit, value, hidden):
        return jnp.where(flips[bit] == value, 1.0, hidden)

    def block_at(b):
        lanes = slab // LANES
        return (
            pl.multiple_of((b // lanes) * TILE_ROWS, TILE_ROWS),
            pl.multiple_of((b % lanes) * LANES, LANES),
        )

    def remains(k):
        own_alpha(k).wait()
        loop(GROUPS - 1, lambda i: recv_alpha(k, i + 1).wait_recv())

        def block(b):
            row, lane = block_at(b)
            place = (pl.ds(row, TILE_ROWS), pl.ds(lane, LANES))
            clear = [1.0 - opac[(k, g) + place].astype(F32) for g in range(GROUPS)]
            eight = [clear[g] * clear[g + 8] for g in range(8)]
            four = [eight[g] * eight[g + 4] for g in range(4)]
            two = [four[g] * four[g + 2] for g in range(2)]
            left = [in_front(0, g, two[1 - g]) for g in range(2)]
            left = [left[g % 2] * in_front(1, g // 2, four[g ^ 2]) for g in range(4)]
            left = [left[g % 4] * in_front(2, g // 4, eight[g ^ 4]) for g in range(8)]
            for g in range(GROUPS):
                left_all[g] = left[g % 8] * in_front(3, g // 8, clear[g ^ 8])
            kept[(k, 0) + place] = left_all[2 * y]
            kept[(k, 1) + place] = left_all[2 * y + 1]
            for j, ends in (((4, 3, 2, 1), 2), ((5, 6, 7), 3)):
                scale = left_all[2 * chip(sigma * j[0])]
                kept[(k, ends) + place] = scale
                scale = 1.0 / scale
                for i in j:
                    for core in range(2):
                        if i != j[0] or core:
                            value = left_all[2 * chip(sigma * i) + core] * scale
                            remain_out[(k, i, core) + place] = (value * value).astype(BF16)

        loop(blocks * (CHUNKS // COARSE), block)
        for j in STEPS:
            send_remain(k, j).start()

    loop(COARSE, remains)

    loop(CHIPS, lambda s: own_colour(s).wait())
    loop(CHIPS, lambda s: recv_colour(s).wait_recv())
    loop(CHIPS, lambda s: send_colour(s).wait_send())
    every(1, GROUPS, lambda k, i: send_alpha(k, i).wait_send())

    def within_coarse(k, row, lane):
        start = (k % (CHUNKS // COARSE)) * chunk + row
        return (pl.ds(pl.multiple_of(start, TILE_ROWS), TILE_ROWS), pl.ds(lane, LANES))

    def add_step(j):
        s = chip(-sigma * j)

        def of_chunk(q, k):
            if j not in (4, 5):
                recv_part(k, j).wait_recv()

            def block(b):
                row, lane = block_at(b)
                place = (pl.ds(row, TILE_ROWS), pl.ds(lane, LANES))
                whole = (pl.ds(pl.multiple_of(k * chunk + row, TILE_ROWS), TILE_ROWS), pl.ds(lane, LANES))
                inner = within_coarse(k, row, lane)
                if j not in (4, 5):
                    first = root(remain_in[(q, j, 0) + inner])
                second = root(remain_in[(q, j, 1) + inner])
                for channel in range(3):
                    total = cols[(0, s, channel) + whole].astype(F32)
                    if j not in (4, 5):
                        total = first * total
                    total += second * cols[(1, s, channel) + whole].astype(F32)
                    if j not in (4, 5):
                        total += root(part_in[(k, j, channel) + place])
                    part_out[(k, j, channel) + place] = square(total)

            loop(blocks, block)
            send_part(k, j).start()

        def at(k):
            if k % (CHUNKS // COARSE) == 0:
                send_remain(k // (CHUNKS // COARSE), j).wait_recv()
            of_chunk(k // (CHUNKS // COARSE), k)

        return at

    def finish(k):
        recv_part(k, 0).wait_recv()
        recv_part(k, 8).wait_recv()

        def block(b):
            row, lane = block_at(b)
            place = (pl.ds(row, TILE_ROWS), pl.ds(lane, LANES))
            whole_row = pl.multiple_of(k * chunk + row, TILE_ROWS)
            whole = (pl.ds(whole_row, TILE_ROWS), pl.ds(lane, LANES))
            middle = (pl.ds(pl.multiple_of(height + whole_row, TILE_ROWS), TILE_ROWS), pl.ds(lane, LANES))
            q = k // (CHUNKS // COARSE)
            inner = within_coarse(k, row, lane)
            first, second = kept[(q, 0) + inner], kept[(q, 1) + inner]
            far, near = kept[(q, 2) + inner], kept[(q, 3) + inner]
            for channel in range(3):
                total = first * cols[(0, y, channel) + whole].astype(F32)
                total += second * cols[(1, y, channel) + whole].astype(F32)
                total += far * root(part_in[(k, 0, channel) + place])
                total += near * root(part_in[(k, 8, channel) + place])
                high = total.astype(BF16)
                window[(channel,) + middle] = high
                low[(channel,) + whole] = (total - high.astype(F32)).astype(BF16)

        loop(blocks, block)
        send_halo(k, 0).start()
        send_halo(k, 1).start()

    bodies = [add_step(j) for j in STEPS] + [finish]
    places = list(range(7)) + [7.8]
    for _, k, i in sorted((places[i] + 0.7 * k, k, i) for i in range(8) for k in range(CHUNKS)):
        bodies[i](k)

    for j in STEPS:
        loop(COARSE, lambda k: send_remain(k, j).wait_send())
        loop(CHUNKS, lambda k: send_part(k, j).wait_send())

    def wait_halo(k):
        send_halo(k, 0).wait_recv()
        send_halo(k, 1).wait_recv()

    def product(a, b):
        return jnp.dot(a, b, preferred_element_type=F32)

    for channel in range(3):
        band = row_picks[:, height : 2 * height]
        partial[channel] = product(band, window[channel, height : 2 * height]) + product(
            band, low[channel]
        )
    loop(CHUNKS, wait_halo)

    for channel in range(3):
        value = partial[channel]
        value += product(row_picks[:, :height], window[channel, :height])
        value += product(row_picks[:, 2 * height :], window[channel, 2 * height :])
        vert[channel, :, HC : HC + slab] = value.astype(BF16)
        for side in range(2):
            send_beside(channel, side).start()
    for channel in range(3):
        partial[channel] = product(
            vert[channel, :, HC : HC + slab], col_matrix[HC : HC + slab]
        )

    within = (t % bands_per_projector) * height + lax.broadcasted_iota(jnp.int32, (height, slab), 0)
    within = within.astype(F32)
    proj_height = bands_per_projector * height
    ramp = jnp.minimum(
        1.0, jnp.minimum((within + 0.5) / BLEND, (proj_height - within - 0.5) / BLEND)
    )

    blended = []
    for channel in range(3):
        for side in range(2):
            send_beside(channel, side).wait_recv()
        value = jnp.concatenate(
            [
                product(vert[channel, :, :HC], col_matrix[:HC, :HC]),
                product(vert[channel, :, HC + slab :], col_matrix[HC + slab :, HC:]),
            ],
            axis=1,
        )
        blended.append((partial[channel] + value) * ramp)
    for channel in range(3):
        mixed = matrix[channel, p, 0] * blended[0]
        mixed += matrix[channel, p, 1] * blended[1]
        mixed += matrix[channel, p, 2] * blended[2]
        out[channel] = mixed + offsets[p, channel]

    loop(CHUNKS, lambda k: send_halo(k, 0).wait_send())
    loop(CHUNKS, lambda k: send_halo(k, 1).wait_send())
    for channel in range(3):
        for side in range(2):
            send_beside(channel, side).wait_send()


def shards(
    colour, alpha, depth_order, row_taps, row_weights, col_taps, col_weights, colour_matrix, offsets
):
    tiles = lax.axis_size("tile")
    height = colour.shape[2]
    slab = colour.shape[3] // GROUPS
    chunk, coarse = height // CHUNKS, height // COARSE
    hbm = pl.BlockSpec(memory_space=pltpu.HBM)
    vmem = pl.BlockSpec(memory_space=pltpu.VMEM)
    matrix = jnp.transpose(colour_matrix, (1, 0, 2))
    dma = pltpu.SemaphoreType.DMA
    return pl.pallas_call(
        functools.partial(kernel, tiles // colour_matrix.shape[0], tiles),
        out_shape=jax.ShapeDtypeStruct((3, height, slab), F32),
        in_specs=[hbm] * 9,
        out_specs=vmem,
        scratch_shapes=[
            pltpu.SMEM(depth_order.shape, depth_order.dtype),
            pltpu.VMEM(row_taps.shape, row_taps.dtype),
            pltpu.VMEM(row_weights.shape, row_weights.dtype),
            pltpu.VMEM(col_taps.shape, col_taps.dtype),
            pltpu.VMEM(col_weights.shape, col_weights.dtype),
            pltpu.SMEM(matrix.shape, matrix.dtype),
            pltpu.SMEM(offsets.shape, offsets.dtype),
            pltpu.VMEM((COARSE, GROUPS, coarse, slab), BF16),
            pltpu.VMEM((2, CHIPS, 3, height, slab), BF16),
            pltpu.VMEM((GROUPS, TILE_ROWS, LANES), F32),
            pltpu.VMEM((COARSE, 4, coarse, slab), F32),
            pltpu.VMEM((COARSE, CHIPS, 2, coarse, slab), BF16),
            pltpu.VMEM((COARSE, CHIPS, 2, coarse, slab), BF16),
            pltpu.VMEM((CHUNKS, CHIPS, 3, chunk, slab), BF16),
            pltpu.VMEM((CHUNKS, CHIPS + 1, 3, chunk, slab), BF16),
            pltpu.VMEM((3, 3 * height, slab), BF16),
            pltpu.VMEM((3, height, slab), BF16),
            pltpu.VMEM((3, height, slab + 2 * HC), BF16),
            pltpu.VMEM((height, 3 * height), BF16),
            pltpu.VMEM((slab + 2 * HC, slab), BF16),
            pltpu.VMEM((3, height, slab), F32),
            dma((COARSE, GROUPS)),
            dma((COARSE, GROUPS)),
            dma((COARSE,)),
            dma((CHIPS,)),
            dma((CHIPS,)),
            dma((CHIPS,)),
            dma((COARSE, CHIPS)),
            dma((COARSE, CHIPS)),
            dma((CHUNKS, CHIPS)),
            dma((CHUNKS, CHIPS + 1)),
            dma((CHUNKS, 2)),
            dma((CHUNKS, 2)),
            dma((3, 2)),
            dma((3, 2)),
            dma((7,)),
        ],
        compiler_params=pltpu.CompilerParams(
            collective_id=0, has_side_effects=True, vmem_limit_bytes=40 * 2**20
        ),
    )(*[
        pltpu.with_memory_space_constraint(x, pltpu.HBM)
        for x in (
            colour, alpha, depth_order, row_taps, row_weights, col_taps, col_weights, matrix, offsets
        )
    ])


def solution(mesh):
    return jax.shard_map(
        shards,
        mesh=mesh,
        in_specs=(
            P("depth", None, "tile", None),
            P("depth", "tile", None),
            P(),
            P(None, "tile"),
            P(None, "tile"),
            P(None, None, "depth"),
            P(None, None, "depth"),
            P(),
            P(),
        ),
        out_specs=P(None, "tile", "depth"),
        check_vma=False,
    )
```

```python
import functools

import jax
import jax.numpy as jnp
from jax import lax
from jax.experimental import pallas as pl
from jax.experimental.pallas import tpu as pltpu
from jax.sharding import PartitionSpec as P

HC = 128
BLEND = 64
GROUPS = 16
CHIPS = 8
CHUNKS = 4
COARSE = 2
TILE_ROWS = 16
LANES = 128
STEPS = (4, 5, 3, 6, 2, 7, 1)
MESH = pl.DeviceIdType.MESH
F32 = jnp.float32
BF16 = jnp.bfloat16


def square(x):
    return (x * jnp.abs(x)).astype(BF16)


def root(v):
    v = v.astype(F32)
    return v * lax.rsqrt(jnp.maximum(jnp.abs(v), 1e-37))


def kernel(
    bands_per_projector,
    tiles,
    colour, alpha, order_in, row_taps_in, row_weights_in, col_taps_in, col_weights_in, matrix_in,
    offsets_in,
    out,
    order, row_taps, row_weights, col_taps, col_weights, matrix, offsets,
    opac, cols, left_all, kept, remain_out, remain_in, part_out, part_in, window, low, vert,
    row_picks, col_matrix, partial,
    a_send, a_recv, a_own, c_own, c_send, c_recv, r_send, r_recv, p_send, p_recv,
    h_send, h_recv, v_send, v_recv, s_own,
):
    height, slab = out.shape[1], out.shape[2]
    chunk = height // CHUNKS
    coarse = height // COARSE
    blocks = (chunk // TILE_ROWS) * (slab // LANES)
    d = lax.axis_index("depth")
    t = lax.axis_index("tile")
    y, c = d // 2, d % 2
    sigma = 1 - 2 * c
    sibling = 2 * y + 1 - c
    below, above = (t + 1) % tiles, (t + tiles - 1) % tiles

    def chip(offset):
        return (y + offset + 2 * CHIPS) % CHIPS

    def columns(device):
        return pl.ds(pl.multiple_of(device * slab, slab), slab)

    def rows_of(k):
        return pl.ds(pl.multiple_of(k * coarse, coarse), coarse)

    barrier = pltpu.get_barrier_semaphore()

    def greet(i, _):
        pl.semaphore_signal(barrier, 1, device_id=((d + i) % GROUPS, t), device_id_type=MESH)
        return 0

    lax.fori_loop(1, GROUPS, greet, 0)
    pl.semaphore_signal(barrier, 1, device_id=(d, below), device_id_type=MESH)
    pl.semaphore_signal(barrier, 1, device_id=(d, above), device_id_type=MESH)

    def own_alpha(k):
        return pltpu.make_async_copy(
            alpha.at[0, rows_of(k), columns(d)], opac.at[k, d], a_own.at[k]
        )

    def own_colour(s):
        return pltpu.make_async_copy(
            colour.at[0, :, :, columns(2 * s + c)], cols.at[c, s], c_own.at[s]
        )

    def loop(n, body):
        def step(i, _):
            body(i)
            return 0

        lax.fori_loop(0, n, step, 0)

    small = [
        pltpu.make_async_copy(source, target, s_own.at[i])
        for i, (source, target) in enumerate((
            (order_in, order),
            (row_taps_in, row_taps),
            (row_weights_in, row_weights),
            (col_taps_in, col_taps),
            (col_weights_in, col_weights),
            (matrix_in, matrix),
            (offsets_in, offsets),
        ))
    ]
    for copy in small:
        copy.start()
    loop(COARSE, lambda k: own_alpha(k).start())
    loop(CHIPS, lambda s: own_colour(s).start())
    pl.semaphore_wait(barrier, GROUPS + 1)

    def send_alpha(k, i):
        to = (d + i) % GROUPS
        return pltpu.make_async_remote_copy(
            src_ref=alpha.at[0, rows_of(k), columns(to)],
            dst_ref=opac.at[k, d],
            send_sem=a_send.at[k, i],
            recv_sem=a_recv.at[k, i],
            device_id=(to, t),
            device_id_type=MESH,
        )

    def recv_alpha(k, i):
        source = (d + GROUPS - i) % GROUPS
        return pltpu.make_async_remote_copy(
            src_ref=alpha.at[0, rows_of(k), columns(source)],
            dst_ref=opac.at[k, source],
            send_sem=a_send.at[k, i],
            recv_sem=a_recv.at[k, i],
            device_id=(source, t),
            device_id_type=MESH,
        )

    def send_colour(s):
        return pltpu.make_async_remote_copy(
            src_ref=colour.at[0, :, :, columns(2 * s + 1 - c)],
            dst_ref=cols.at[c, s],
            send_sem=c_send.at[s],
            recv_sem=c_recv.at[s],
            device_id=(sibling, t),
            device_id_type=MESH,
        )

    def recv_colour(s):
        return pltpu.make_async_remote_copy(
            src_ref=colour.at[0, :, :, columns(2 * s + 1 - c)],
            dst_ref=cols.at[1 - c, s],
            send_sem=c_send.at[s],
            recv_sem=c_recv.at[s],
            device_id=(sibling, t),
            device_id_type=MESH,
        )

    def send_remain(k, j):
        to = chip(sigma * j)
        first = 1 if j in (4, 5) else 0
        return pltpu.make_async_remote_copy(
            src_ref=remain_out.at[k, j, pl.ds(first, 2 - first)],
            dst_ref=remain_in.at[k, j, pl.ds(first, 2 - first)],
            send_sem=r_send.at[k, j],
            recv_sem=r_recv.at[k, j],
            device_id=(2 * to + c, t),
            device_id_type=MESH,
        )

    def send_part(k, j):
        to = chip(-sigma) if j <= 4 else chip(sigma)
        return pltpu.make_async_remote_copy(
            src_ref=part_out.at[k, j],
            dst_ref=part_in.at[k, j - 1 if j <= 4 else j + 1],
            send_sem=p_send.at[k, j],
            recv_sem=p_recv.at[k, j - 1 if j <= 4 else j + 1],
            device_id=(2 * to + c, t),
            device_id_type=MESH,
        )

    def recv_part(k, slot):
        return pltpu.make_async_remote_copy(
            src_ref=part_out.at[k, 1],
            dst_ref=part_in.at[k, slot],
            send_sem=p_send.at[k, 1],
            recv_sem=p_recv.at[k, slot],
            device_id=(sibling, t),
            device_id_type=MESH,
        )

    def send_halo(k, side):
        middle = window.at[:, pl.ds(pl.multiple_of(height + k * chunk, chunk), chunk), :]
        at = 2 * height if side == 0 else 0
        return pltpu.make_async_remote_copy(
            src_ref=middle,
            dst_ref=window.at[:, pl.ds(pl.multiple_of(at + k * chunk, chunk), chunk), :],
            send_sem=h_send.at[k, side],
            recv_sem=h_recv.at[k, side],
            device_id=(d, above if side == 0 else below),
            device_id_type=MESH,
        )

    def send_beside(channel, side):
        to = (d + GROUPS - 1) % GROUPS if side == 0 else (d + 1) % GROUPS
        source = HC if side == 0 else slab
        target = HC + slab if side == 0 else 0
        return pltpu.make_async_remote_copy(
            src_ref=vert.at[channel, :, pl.ds(source, HC)],
            dst_ref=vert.at[channel, :, pl.ds(target, HC)],
            send_sem=v_send.at[channel, side],
            recv_sem=v_recv.at[channel, side],
            device_id=(to, t),
            device_id_type=MESH,
        )

    def every(first, last, body):
        def outer(k, _):
            def inner(i, _):
                body(k, i)
                return 0

            return lax.fori_loop(first, last, inner, 0)

        lax.fori_loop(0, COARSE, outer, 0)

    every(1, GROUPS, lambda k, i: send_alpha(k, i).start())
    loop(CHIPS, lambda s: send_colour(s).start())

    for copy in small:
        copy.wait()
    flips = [(order[0] // (1 << bit)) % 2 for bit in range(4)]

    place = lax.broadcasted_iota(jnp.int32, (3 * height, height), 0)
    picks = jnp.zeros((3 * height, height), F32)
    for tap in range(4):
        taps = row_taps[tap, :][None, :]
        picks += jnp.where(taps == place, row_weights[tap, :].astype(F32)[None, :], 0.0)
    outside = ((place < height) & (t == 0)) | ((place >= 2 * height) & (t == tiles - 1))
    row_picks[...] = jnp.transpose(jnp.where(outside, 0.0, picks)).astype(BF16)

    width = slab + 2 * HC
    p = t // bands_per_projector
    place = lax.broadcasted_iota(jnp.int32, (width, slab), 0) + (d * slab - HC)
    col_picks = jnp.zeros((width, slab), F32)
    for tap in range(4):
        taps = col_taps[p, tap, :][None, :]
        col_picks += jnp.where(taps == place, col_weights[p, tap, :].astype(F32)[None, :], 0.0)
    col_matrix[...] = col_picks.astype(BF16)


    def in_front(bit, value, hidden):
        return jnp.where(flips[bit] == value, 1.0, hidden)

    def block_at(b):
        lanes = slab // LANES
        return (
            pl.multiple_of((b // lanes) * TILE_ROWS, TILE_ROWS),
            pl.multiple_of((b % lanes) * LANES, LANES),
        )

    def remains(k):
        own_alpha(k).wait()
        loop(GROUPS - 1, lambda i: recv_alpha(k, i + 1).wait_recv())

        def block(b):
            row, lane = block_at(b)
            place = (pl.ds(row, TILE_ROWS), pl.ds(lane, LANES))
            clear = [1.0 - opac[(k, g) + place].astype(F32) for g in range(GROUPS)]
            eight = [clear[g] * clear[g + 8] for g in range(8)]
            four = [eight[g] * eight[g + 4] for g in range(4)]
            two = [four[g] * four[g + 2] for g in range(2)]
            left = [in_front(0, g, two[1 - g]) for g in range(2)]
            left = [left[g % 2] * in_front(1, g // 2, four[g ^ 2]) for g in range(4)]
            left = [left[g % 4] * in_front(2, g // 4, eight[g ^ 4]) for g in range(8)]
            for g in range(GROUPS):
                left_all[g] = left[g % 8] * in_front(3, g // 8, clear[g ^ 8])
            kept[(k, 0) + place] = left_all[2 * y]
            kept[(k, 1) + place] = left_all[2 * y + 1]
            for j, ends in (((4, 3, 2, 1), 2), ((5, 6, 7), 3)):
                scale = left_all[2 * chip(sigma * j[0])]
                kept[(k, ends) + place] = scale
                scale = 1.0 / scale
                for i in j:
                    for core in range(2):
                        if i != j[0] or core:
                            value = left_all[2 * chip(sigma * i) + core] * scale
                            remain_out[(k, i, core) + place] = (value * value).astype(BF16)

        loop(blocks * (CHUNKS // COARSE), block)
        for j in STEPS:
            send_remain(k, j).start()

    loop(COARSE, remains)

    loop(CHIPS, lambda s: own_colour(s).wait())
    loop(CHIPS, lambda s: recv_colour(s).wait_recv())
    loop(CHIPS, lambda s: send_colour(s).wait_send())
    every(1, GROUPS, lambda k, i: send_alpha(k, i).wait_send())

    def within_coarse(k, row, lane):
        start = (k % (CHUNKS // COARSE)) * chunk + row
        return (pl.ds(pl.multiple_of(start, TILE_ROWS), TILE_ROWS), pl.ds(lane, LANES))

    def add_step(j):
        s = chip(-sigma * j)

        def of_chunk(q, k):
            if j not in (4, 5):
                recv_part(k, j).wait_recv()

            def block(b):
                row, lane = block_at(b)
                place = (pl.ds(row, TILE_ROWS), pl.ds(lane, LANES))
                whole = (pl.ds(pl.multiple_of(k * chunk + row, TILE_ROWS), TILE_ROWS), pl.ds(lane, LANES))
                inner = within_coarse(k, row, lane)
                if j not in (4, 5):
                    first = root(remain_in[(q, j, 0) + inner])
                second = root(remain_in[(q, j, 1) + inner])
                for channel in range(3):
                    total = cols[(0, s, channel) + whole].astype(F32)
                    if j not in (4, 5):
                        total = first * total
                    total += second * cols[(1, s, channel) + whole].astype(F32)
                    if j not in (4, 5):
                        total += root(part_in[(k, j, channel) + place])
                    part_out[(k, j, channel) + place] = square(total)

            loop(blocks, block)
            send_part(k, j).start()

        def at(k):
            if k % (CHUNKS // COARSE) == 0:
                send_remain(k // (CHUNKS // COARSE), j).wait_recv()
            of_chunk(k // (CHUNKS // COARSE), k)

        return at

    bodies = [add_step(j) for j in STEPS]
    for _, k, i in sorted((i + 0.7 * k, k, i) for i in range(7) for k in range(CHUNKS)):
        bodies[i](k)

    def finish(k):
        recv_part(k, 0).wait_recv()
        recv_part(k, 8).wait_recv()

        def block(b):
            row, lane = block_at(b)
            place = (pl.ds(row, TILE_ROWS), pl.ds(lane, LANES))
            whole_row = pl.multiple_of(k * chunk + row, TILE_ROWS)
            whole = (pl.ds(whole_row, TILE_ROWS), pl.ds(lane, LANES))
            middle = (pl.ds(pl.multiple_of(height + whole_row, TILE_ROWS), TILE_ROWS), pl.ds(lane, LANES))
            q = k // (CHUNKS // COARSE)
            inner = within_coarse(k, row, lane)
            first, second = kept[(q, 0) + inner], kept[(q, 1) + inner]
            far, near = kept[(q, 2) + inner], kept[(q, 3) + inner]
            for channel in range(3):
                total = first * cols[(0, y, channel) + whole].astype(F32)
                total += second * cols[(1, y, channel) + whole].astype(F32)
                total += far * root(part_in[(k, 0, channel) + place])
                total += near * root(part_in[(k, 8, channel) + place])
                high = total.astype(BF16)
                window[(channel,) + middle] = high
                low[(channel,) + whole] = (total - high.astype(F32)).astype(BF16)

        loop(blocks, block)
        send_halo(k, 0).start()
        send_halo(k, 1).start()

    loop(CHUNKS, finish)

    for j in STEPS:
        loop(COARSE, lambda k: send_remain(k, j).wait_send())
        loop(CHUNKS, lambda k: send_part(k, j).wait_send())

    def wait_halo(k):
        send_halo(k, 0).wait_recv()
        send_halo(k, 1).wait_recv()

    def product(a, b):
        return jnp.dot(a, b, preferred_element_type=F32)

    for channel in range(3):
        band = row_picks[:, height : 2 * height]
        partial[channel] = product(band, window[channel, height : 2 * height]) + product(
            band, low[channel]
        )
    loop(CHUNKS, wait_halo)

    for channel in range(3):
        value = partial[channel]
        value += product(row_picks[:, :height], window[channel, :height])
        value += product(row_picks[:, 2 * height :], window[channel, 2 * height :])
        vert[channel, :, HC : HC + slab] = value.astype(BF16)
        for side in range(2):
            send_beside(channel, side).start()
    for channel in range(3):
        partial[channel] = product(
            vert[channel, :, HC : HC + slab], col_matrix[HC : HC + slab]
        )

    within = (t % bands_per_projector) * height + lax.broadcasted_iota(jnp.int32, (height, slab), 0)
    within = within.astype(F32)
    proj_height = bands_per_projector * height
    ramp = jnp.minimum(
        1.0, jnp.minimum((within + 0.5) / BLEND, (proj_height - within - 0.5) / BLEND)
    )

    blended = []
    for channel in range(3):
        for side in range(2):
            send_beside(channel, side).wait_recv()
        value = jnp.concatenate(
            [
                product(vert[channel, :, :HC], col_matrix[:HC, :HC]),
                product(vert[channel, :, HC + slab :], col_matrix[HC + slab :, HC:]),
            ],
            axis=1,
        )
        blended.append((partial[channel] + value) * ramp)
    for channel in range(3):
        mixed = matrix[channel, p, 0] * blended[0]
        mixed += matrix[channel, p, 1] * blended[1]
        mixed += matrix[channel, p, 2] * blended[2]
        out[channel] = mixed + offsets[p, channel]

    loop(CHUNKS, lambda k: send_halo(k, 0).wait_send())
    loop(CHUNKS, lambda k: send_halo(k, 1).wait_send())
    for channel in range(3):
        for side in range(2):
            send_beside(channel, side).wait_send()


def shards(
    colour, alpha, depth_order, row_taps, row_weights, col_taps, col_weights, colour_matrix, offsets
):
    tiles = lax.axis_size("tile")
    height = colour.shape[2]
    slab = colour.shape[3] // GROUPS
    chunk, coarse = height // CHUNKS, height // COARSE
    hbm = pl.BlockSpec(memory_space=pltpu.HBM)
    vmem = pl.BlockSpec(memory_space=pltpu.VMEM)
    matrix = jnp.transpose(colour_matrix, (1, 0, 2))
    dma = pltpu.SemaphoreType.DMA
    return pl.pallas_call(
        functools.partial(kernel, tiles // colour_matrix.shape[0], tiles),
        out_shape=jax.ShapeDtypeStruct((3, height, slab), F32),
        in_specs=[hbm] * 9,
        out_specs=vmem,
        scratch_shapes=[
            pltpu.SMEM(depth_order.shape, depth_order.dtype),
            pltpu.VMEM(row_taps.shape, row_taps.dtype),
            pltpu.VMEM(row_weights.shape, row_weights.dtype),
            pltpu.VMEM(col_taps.shape, col_taps.dtype),
            pltpu.VMEM(col_weights.shape, col_weights.dtype),
            pltpu.SMEM(matrix.shape, matrix.dtype),
            pltpu.SMEM(offsets.shape, offsets.dtype),
            pltpu.VMEM((COARSE, GROUPS, coarse, slab), BF16),
            pltpu.VMEM((2, CHIPS, 3, height, slab), BF16),
            pltpu.VMEM((GROUPS, TILE_ROWS, LANES), F32),
            pltpu.VMEM((COARSE, 4, coarse, slab), F32),
            pltpu.VMEM((COARSE, CHIPS, 2, coarse, slab), BF16),
            pltpu.VMEM((COARSE, CHIPS, 2, coarse, slab), BF16),
            pltpu.VMEM((CHUNKS, CHIPS, 3, chunk, slab), BF16),
            pltpu.VMEM((CHUNKS, CHIPS + 1, 3, chunk, slab), BF16),
            pltpu.VMEM((3, 3 * height, slab), BF16),
            pltpu.VMEM((3, height, slab), BF16),
            pltpu.VMEM((3, height, slab + 2 * HC), BF16),
            pltpu.VMEM((height, 3 * height), BF16),
            pltpu.VMEM((slab + 2 * HC, slab), BF16),
            pltpu.VMEM((3, height, slab), F32),
            dma((COARSE, GROUPS)),
            dma((COARSE, GROUPS)),
            dma((COARSE,)),
            dma((CHIPS,)),
            dma((CHIPS,)),
            dma((CHIPS,)),
            dma((COARSE, CHIPS)),
            dma((COARSE, CHIPS)),
            dma((CHUNKS, CHIPS)),
            dma((CHUNKS, CHIPS + 1)),
            dma((CHUNKS, 2)),
            dma((CHUNKS, 2)),
            dma((3, 2)),
            dma((3, 2)),
            dma((7,)),
        ],
        compiler_params=pltpu.CompilerParams(
            collective_id=0, has_side_effects=True, vmem_limit_bytes=40 * 2**20
        ),
    )(*[
        pltpu.with_memory_space_constraint(x, pltpu.HBM)
        for x in (
            colour, alpha, depth_order, row_taps, row_weights, col_taps, col_weights, matrix, offsets
        )
    ])


def solution(mesh):
    return jax.shard_map(
        shards,
        mesh=mesh,
        in_specs=(
            P("depth", None, "tile", None),
            P("depth", "tile", None),
            P(),
            P(None, "tile"),
            P(None, "tile"),
            P(None, None, "depth"),
            P(None, None, "depth"),
            P(),
            P(),
        ),
        out_specs=P(None, "tile", "depth"),
        check_vma=False,
    )
```
